256 devices in a mesh: gx: 16 (over x, z_lo), gy: 16 (over y, z_hi, core).
Axes of the slice: x: 4, y: 4, z: 8 (z_hi: 2, z_lo: 4; z = z_hi * 4 + z_lo), core: 2. Of those that a mesh axis runs over, the one named last changes fastest.
Arguments:
- positions: float32 [16, 16, 3, 256], P('gx', 'gy'), may hold values from 0 to 1
- velocities: float32 [16, 16, 3, 256], P('gx', 'gy'), may hold values from -4 to 4
- species: int32 [16, 16, 256], P('gx', 'gy'), may hold values from 0 to 4
- edge_center: int32 [16, 16, 512], P('gx', 'gy'), may hold values from 0 to 255
- edge_neighbor: int32 [16, 16, 512], P('gx', 'gy'), may hold values from 0 to 767, as said below
- edge_count: int32 [16, 16], P('gx', 'gy'), may hold values from 256 to 512, as said below
- ghost_lists: int32 [16, 16, 4, 128], P('gx', 'gy'), may hold values from 0 to 255
- migrate_lists: int32 [16, 16, 4, 16], P('gx', 'gy'), may hold values from 0 to 255, as said below
- radial_weight: float32 [8, 64], replicated, may hold values from -2 to 2
- center_embed: float32 [5, 64], replicated, may hold values from -4 to 4
- neighbor_embed: float32 [5, 64], replicated, may hold values from -4 to 4
- product_weight: float32 [2, 64, 192], replicated, may hold values from -0.75 to 0.75
- mixer_in: float32 [2, 256, 64], replicated, may hold values from -0.375 to 0.375
- mixer_out: float32 [2, 64, 64], replicated, may hold values from -0.75 to 0.75
- feature_weight: float32 [64, 64], replicated, may hold values from -0.75 to 0.75
- energy_head: float32 [64], replicated, may hold values from -0.75 to 0.75
Outputs:
- forces: float32 [16, 16, 3, 256], P('gx', 'gy')
- new_positions: float32 [16, 16, 3, 256], P('gx', 'gy')
- new_velocities: float32 [16, 16, 3, 256], P('gx', 'gy')
The draws below stay inside these ranges and needn't reach their ends.
Inputs may be any that keep to these rules, and one draw needn't show every extreme that they name: `edge_neighbor`: never equal to the edge's centre. `edge_count`: some domain uses all 512 slots in every draw. `migrate_lists`: all 64 entries of one domain differ.
All inputs are finite; a program needn't handle non-finite values.
Results may differ from the reference program's by a relative error of at most 0.0003.
Values sent between devices are 32-bit elements; how exact they have to be, the bound alone decides.
A program may use at most 128 MiB of HBM per device.

```python
import jax
import jax.numpy as jnp
from jax import lax

CHANNELS = 64
BASIS = 8
SPECIES = 5
LAYERS = 2
ATOMS = 256
GHOST = 128
EDGES = 512
MIGRANTS = 16
DOM_X = 16
DOM_Y = 16


def edge_pairs(key):
    center = jax.random.randint(jax.random.fold_in(key, 11), (DOM_X, DOM_Y, EDGES), 0, ATOMS)
    offset_draw = jax.random.randint(jax.random.fold_in(key, 12), (DOM_X, DOM_Y, EDGES), 1, ATOMS + 4 * GHOST)
    return (center, (center + offset_draw) % (ATOMS + 4 * GHOST))


def draw_edge_center(key, part):
    return edge_pairs(key)[0]


def draw_edge_neighbor(key, part):
    return edge_pairs(key)[1]


def draw_edge_count(key, part):
    key = jax.random.fold_in(key, 3)
    upper = EDGES - EDGES // 2
    first_draw = jax.random.randint(jax.random.fold_in(key, 1), (DOM_X * DOM_Y,), 0, upper)
    second_draw = jax.random.randint(jax.random.fold_in(key, 2), (DOM_X * DOM_Y,), 0, upper)
    counts = EDGES // 2 + first_draw * second_draw // upper
    busiest = jax.random.randint(jax.random.fold_in(key, 4), (), 0, DOM_X * DOM_Y)
    flattened = counts.at[busiest].set(EDGES)
    return flattened.reshape(DOM_X, DOM_Y)


def draw_migrate_lists(key, part):
    key = jax.random.fold_in(key, 5)
    key_list = jax.random.split(key, DOM_X * DOM_Y)

    def pick_some(single_key):
        return jax.random.permutation(single_key, ATOMS)[0:4 * MIGRANTS].astype(jnp.int32)
    chosen = jax.vmap(pick_some)(key_list)
    return chosen.reshape(DOM_X, DOM_Y, 4, MIGRANTS)


def place_ends(result, stream_key, least, largest):
    dims = result.shape
    index_at = [jax.random.randint(jax.random.fold_in(stream_key, axis), (), 0, dims[axis]) for axis in range(len(dims))]
    result = result.at[tuple(index_at)].set(least)
    longest = dims.index(max(dims))
    index_at[longest] = (index_at[longest] + 1) % dims[longest]
    return result.at[tuple(index_at)].set(largest)


def shard_levels(rng, dims, pieces, low, top_value):
    def one(position, blocks):
        draws = jax.random.uniform(jax.random.fold_in(jax.random.fold_in(rng, 6), position), (blocks,), jnp.float32, low / len(pieces), top_value / len(pieces))
        return jnp.repeat(jnp.exp(draws), dims[position] // blocks).reshape((-1,) + (1,) * (len(dims) - position - 1))

    gain = one(*pieces[0])
    for cut in pieces[1:]:
        gain = gain * one(*cut)
    return gain


def noise(own_key, shape, width, limit, cuts=(), kind=jnp.bfloat16):
    drawn = width * jax.random.normal(own_key, shape, jnp.float32)
    if cuts:
        drawn = drawn * shard_levels(own_key, shape, cuts, -0.22, 0.18)
    return jnp.clip(drawn, -limit, limit).astype(kind)


def setup_inputs(seed: int = 0) -> dict:
    keys = jax.random.split(jax.random.key(seed), 17)
    return {
        "positions": jnp.clip(1.0 * jax.random.uniform(keys[0], (DOM_X, DOM_Y, 3, ATOMS), jnp.float32) ** shard_levels(keys[0], (DOM_X, DOM_Y, 3, ATOMS), ((0, 16), (1, 16)), -0.2, 0.2), 0.0, 1.0),
        "velocities": noise(keys[1], (DOM_X, DOM_Y, 3, ATOMS), 1.0, 4.0, ((0, 16), (1, 16)), jnp.float32),
        "species": place_ends(jax.random.randint(keys[2], (DOM_X, DOM_Y, ATOMS), 0, SPECIES), jax.random.fold_in(keys[2], 1), 0, SPECIES - 1).astype(jnp.int32),
        "edge_center": draw_edge_center(jax.random.fold_in(keys[16], 71), 0),
        "edge_neighbor": draw_edge_neighbor(jax.random.fold_in(keys[16], 71), 0),
        "edge_count": draw_edge_count(jax.random.fold_in(keys[16], 71), 0),
        "ghost_lists": place_ends(jax.random.randint(keys[6], (DOM_X, DOM_Y, 4, GHOST), 0, ATOMS), jax.random.fold_in(keys[6], 1), 0, ATOMS - 1).astype(jnp.int32),
        "migrate_lists": draw_migrate_lists(jax.random.fold_in(keys[16], 71), 0),
        "radial_weight": noise(keys[8], (BASIS, CHANNELS), BASIS ** -0.5, 2.0, (), jnp.float32),
        "center_embed": noise(keys[9], (SPECIES, CHANNELS), 1.0, 4.0, (), jnp.float32),
        "neighbor_embed": noise(keys[10], (SPECIES, CHANNELS), 1.0, 4.0, (), jnp.float32),
        "product_weight": noise(keys[11], (LAYERS, CHANNELS, 3 * CHANNELS), CHANNELS ** -0.5, 0.75, (), jnp.float32),
        "mixer_in": noise(keys[12], (LAYERS, 4 * CHANNELS, CHANNELS), (4 * CHANNELS) ** -0.5, 0.375, (), jnp.float32),
        "mixer_out": noise(keys[13], (LAYERS, CHANNELS, CHANNELS), CHANNELS ** -0.5, 0.75, (), jnp.float32),
        "feature_weight": noise(keys[14], (CHANNELS, CHANNELS), CHANNELS ** -0.5, 0.75, (), jnp.float32),
        "energy_head": noise(keys[15], (CHANNELS,), CHANNELS ** -0.5, 0.75, (), jnp.float32),
    }


ENV_SCALE = 0.5
SOFTENING = 0.04
STEP_TIME = 0.1
BASIS_WIDTH = 0.4
BASIS_REACH = 2.5
INVERSE_MASS = (0.992063, 0.083257, 0.071393, 0.062504, 0.031192)
FRAME_SHIFT = ((1.0, 0.0), (-1.0, 0.0), (0.0, 1.0), (0.0, -1.0))
ROOT_THREE = 3.0 ** 0.5
ROOT_FIVE = 5.0 ** 0.5
ROOT_FIFTEEN = 15.0 ** 0.5

def contract(weight, values):
    return lax.dot_general(weight, values, (((0,), (0,)), ((), ())), precision=lax.Precision.HIGHEST, preferred_element_type=jnp.float32)

def harmonics(unit_vec):
    unit_x, unit_y, unit_z = (unit_vec[0], unit_vec[1], unit_vec[2])
    return jnp.stack([jnp.ones_like(unit_x), ROOT_THREE * unit_x, ROOT_THREE * unit_y, ROOT_THREE * unit_z, ROOT_FIFTEEN * unit_x * unit_y, ROOT_FIFTEEN * unit_y * unit_z, 0.5 * ROOT_FIVE * (3.0 * unit_z * unit_z - 1.0), ROOT_FIFTEEN * unit_x * unit_z, 0.5 * ROOT_FIFTEEN * (unit_x * unit_x - unit_y * unit_y)])

def one_hot(value_row, level_count):
    levels = jnp.arange(level_count).astype(jnp.float32)
    return (value_row[None, :] == levels[:, None]).astype(jnp.float32)

def edge_layer(hidden, harmonic, center, weight_mask, atom_count, product_weight, mixer_in, mixer_out):
    channels = hidden.shape[0]
    coupled = contract(product_weight, hidden).reshape(3, channels, -1)
    features = jnp.concatenate([coupled[0:1] * harmonic[0:1, None, :], coupled[1:2] * harmonic[1:4, None, :], coupled[2:3] * harmonic[4:9, None, :]], axis=0)
    environ = jnp.zeros((9, channels, atom_count), jnp.float32).at[:, :, center].add(features * weight_mask) * ENV_SCALE
    paired = features * environ[:, :, center]
    invariant = jnp.concatenate([paired[0], lax.optimization_barrier(jnp.sum(paired[1:4], axis=0)), lax.optimization_barrier(jnp.sum(paired[4:9], axis=0))], axis=0)
    joined = jnp.concatenate([hidden, invariant], axis=0)
    return hidden + contract(mixer_out, jax.nn.silu(contract(mixer_in, joined)))

def first_half(extended, center, neighbor, weight_mask, atom_count, radial_weight, center_embed, neighbor_embed, product_weight, mixer_in, mixer_out):
    center_rows = extended[:, center]
    neighbor_rows = extended[:, neighbor]
    separation = neighbor_rows[0:3] - center_rows[0:3]
    length = jnp.sqrt(lax.optimization_barrier(jnp.sum(separation * separation, axis=0)) + SOFTENING)
    harmonic = harmonics(separation / length)
    basis_count = radial_weight.shape[0]
    centres = BASIS_REACH * jnp.arange(basis_count).astype(jnp.float32) / (basis_count - 1)
    radial_basis = jnp.exp(-jnp.square((length[None, :] - centres[:, None]) / BASIS_WIDTH))
    species_count = center_embed.shape[0]
    initial = jax.nn.silu(contract(radial_weight, radial_basis) + contract(center_embed, one_hot(center_rows[3], species_count)) + contract(neighbor_embed, one_hot(neighbor_rows[3], species_count)))
    hidden = edge_layer(initial, harmonic, center, weight_mask, atom_count, product_weight[0], mixer_in[0], mixer_out[0])
    summary = jnp.zeros((hidden.shape[0], atom_count), jnp.float32).at[:, center].add(hidden * weight_mask) * ENV_SCALE
    return (summary, hidden, harmonic)

def second_half(harmonic, hidden, projected, center, neighbor, weight_mask, atom_count, product_weight, mixer_in, mixer_out, energy_head):
    combined = hidden + projected[:, neighbor]
    last_hidden = edge_layer(combined, harmonic, center, weight_mask, atom_count, product_weight[1], mixer_in[1], mixer_out[1])
    return jnp.sum(contract(energy_head[:, None], last_hidden)[0] * weight_mask)

def pick_columns(stack_rows, lists):

    def single(block_rows, index_list):
        return block_rows[:, index_list]
    return jax.vmap(jax.vmap(single))(stack_rows, lists)

def place_columns(block_rows, index_list, values):
    return block_rows.at[:, index_list].set(values)

def from_faces(sent_rows):
    return [jnp.roll(sent_rows[0], 1, axis=0), jnp.roll(sent_rows[1], -1, axis=0), jnp.roll(sent_rows[2], 1, axis=1), jnp.roll(sent_rows[3], -1, axis=1)]

def to_frame(block_rows, face_index):
    return block_rows.at[:, :, 0].add(-FRAME_SHIFT[face_index][0]).at[:, :, 1].add(-FRAME_SHIFT[face_index][1])

def reference(positions, velocities, species, edge_center, edge_neighbor, edge_count, ghost_lists, migrate_lists, radial_weight, center_embed, neighbor_embed, product_weight, mixer_in, mixer_out, feature_weight, energy_head):
    grid_x = positions.shape[0]
    grid_y = positions.shape[1]
    atom_count = positions.shape[3]
    edge_total = edge_center.shape[2]
    edge_masks = (jnp.arange(edge_total)[None, None, :] < edge_count[:, :, None]).astype(jnp.float32)
    species_value = species.astype(jnp.float32)

    def flatten_grid(array):
        return array.reshape((grid_x * grid_y,) + array.shape[2:])

    def front_domain(operands):
        extended, center, neighbor, weight_mask = operands
        return first_half(extended, center, neighbor, weight_mask, atom_count, radial_weight, center_embed, neighbor_embed, product_weight, mixer_in, mixer_out)[0]

    def whole_domain(operands):
        extended, summaries, center, neighbor, weight_mask = operands
        summary, hidden, harmonic = first_half(extended, center, neighbor, weight_mask, atom_count, radial_weight, center_embed, neighbor_embed, product_weight, mixer_in, mixer_out)
        return second_half(harmonic, hidden, contract(feature_weight, summaries), center, neighbor, weight_mask, atom_count, product_weight, mixer_in, mixer_out, energy_head)

    def total_energy(coords):
        stacked = jnp.concatenate([coords, species_value[:, :, None, :]], axis=2)
        sent_rows = [to_frame(pick_columns(stacked, ghost_lists[:, :, face_index]), face_index) for face_index in range(4)]
        extended = jnp.concatenate([stacked] + from_faces(sent_rows), axis=3)
        summary = lax.map(jax.checkpoint(front_domain), (flatten_grid(extended), flatten_grid(edge_center), flatten_grid(edge_neighbor), flatten_grid(edge_masks)))
        summary = summary.reshape((grid_x, grid_y) + summary.shape[1:])
        lent = from_faces([pick_columns(summary, ghost_lists[:, :, face_index]) for face_index in range(4)])
        shared = jnp.concatenate([summary] + lent, axis=3)
        energies = lax.map(jax.checkpoint(whole_domain), (flatten_grid(extended), flatten_grid(shared), flatten_grid(edge_center), flatten_grid(edge_neighbor), flatten_grid(edge_masks)))
        return jnp.sum(energies)
    forces = -jax.grad(total_energy)(positions)
    mass_table = jnp.array(INVERSE_MASS, jnp.float32)
    inverse = lax.optimization_barrier(jnp.sum((species[:, :, :, None] == jnp.arange(mass_table.shape[0])).astype(jnp.float32) * mass_table, axis=3))
    stepped_velocities = velocities + STEP_TIME * forces * inverse[:, :, None, :]
    stepped_positions = positions + STEP_TIME * stepped_velocities
    atom_state = jnp.concatenate([stepped_positions, stepped_velocities], axis=2)
    moving = from_faces([to_frame(pick_columns(atom_state, migrate_lists[:, :, face_index]), face_index) for face_index in range(4)])
    for face_index in range(4):
        atom_state = jax.vmap(jax.vmap(place_columns))(atom_state, migrate_lists[:, :, face_index], moving[face_index])
    return (forces, atom_state[:, :, 0:3], atom_state[:, :, 3:6])
```

```python
import functools

import jax
import jax.numpy as jnp
from jax import lax
from jax.experimental import pallas as pl
from jax.experimental.pallas import tpu as pltpu
from jax.sharding import PartitionSpec as P

F32 = jnp.float32
BF16 = jnp.bfloat16
ENV_SCALE = 0.5
SOFTENING = 0.04
STEP_TIME = 0.1
BASIS_WIDTH = 0.4
BASIS_REACH = 2.5
INVERSE_MASS = (0.992063, 0.083257, 0.071393, 0.062504, 0.031192)
ROOT_THREE = 3.0**0.5
ROOT_FIVE = 5.0**0.5
ROOT_FIFTEEN = 15.0**0.5
ATOMS = 256
GHOST = 128
EDGES = 512
CH = 64
MIG = 16


def split2(x):
    hi = x.astype(BF16)
    return hi, (x - hi.astype(F32)).astype(BF16)


def split2f(x):
    hi = x.astype(BF16).astype(F32)
    return hi, x - hi


def split3f(x):
    hi = x.astype(BF16).astype(F32)
    rest = x - hi
    mid = rest.astype(BF16).astype(F32)
    return hi, mid, rest - mid


def mm(a, b):
    return lax.dot_general(a, b, (((1,), (0,)), ((), ())), preferred_element_type=F32)


def mm_nt(a, b):
    return lax.dot_general(a, b, (((1,), (1,)), ((), ())), preferred_element_type=F32)


def mm_tn(a, b):
    return lax.dot_general(a, b, (((0,), (0,)), ((), ())), preferred_element_type=F32)


def stack4(x):
    hi, lo = split2(x)
    return jnp.concatenate([hi, hi, lo, lo], axis=0)


def split3(x):
    hi = x.astype(BF16)
    rest = x - hi.astype(F32)
    mid = rest.astype(BF16)
    return hi, mid, (rest - mid.astype(F32)).astype(BF16)


def stack6(x):
    hi, mid, lo = split3(x)
    return jnp.concatenate([hi, mid, lo, hi, mid, hi], axis=0)


def exact_rows(x, hot, product):
    hi, mid, lo = split3f(x)
    parts = jnp.concatenate([hi, mid, lo, jnp.zeros_like(lo)], axis=0).astype(BF16)
    out = product(parts, hot)
    return out[0:8] + out[8:16] + out[16:24]


def many_rows(x, hot, product):
    rows = x.shape[0]
    out = product(jnp.concatenate(split3(x), axis=0), hot)
    return out[0:rows] + (out[rows:2 * rows] + out[2 * rows:])


def wide4(w):
    hi, lo = split2f(w)
    return jnp.concatenate([hi, lo, hi, lo], axis=1).astype(BF16)


def wide4_t(w):
    hi, lo = split2f(w)
    return jnp.transpose(jnp.concatenate([hi, lo, hi, lo], axis=0)).astype(BF16)


def wide6_t(w):
    hi, mid, lo = split3f(w)
    return jnp.transpose(jnp.concatenate([hi, hi, hi, mid, mid, lo], axis=0)).astype(BF16)


def tall2(w):
    hi, lo = split2f(w)
    return jnp.concatenate([hi, lo], axis=0).astype(BF16)


def tall3(w):
    return jnp.concatenate(split3f(w), axis=0).astype(BF16)


def mm_tall2(w2, x):
    rows = w2.shape[0] // 2
    hi, lo = split2(x)
    out = mm(w2, hi)
    small = mm(w2, lo)
    return out[0:rows] + (out[rows:] + small[0:rows] + small[rows:])


def mm_tall3(w3, x):
    rows = w3.shape[0] // 3
    hi, mid, lo = split3(x)
    first = mm(w3, hi)
    second = mm(w3[0:2 * rows], mid)
    third = mm(w3[0:rows], lo)
    return first[0:rows] + (
        first[rows:2 * rows] + second[0:rows] + (first[2 * rows:] + second[rows:] + third)
    )


def kernel(
    nx, ny,
    pos_in, vel_in, spec_in, cen_in, nei_in, cnt_in, gl_in, ml_in,
    wr_in, ce_in, ne_in, pw_in, mi_in, mo_in, fw_in, eh_in,
    home,
    f_out, p_out, v_out,
    pos_ref, vel_ref, spec_ref, cen_ref, nei_ref, cnt_ref, gl_ref, ml_ref,
    wr_ref, ce_ref, ne_ref, pw_ref, mi_ref, mo_ref, fw_ref, eh_ref,
    stk, wbase, k0, k1h, k1l, k2h, k2l, lmat, mmat, nghost, ghot, dhot, psum1, psum2, yrow, grow,
    s1, r1, s2, r2, s3, r3, s4, r4, s5, r5, ssem, rsem, lsem, osem,
):
    mx = lax.axis_index("gx")
    my = lax.axis_index("gy")
    toward = (
        (lax.rem(mx + 1, nx), my),
        (lax.rem(mx + nx - 1, nx), my),
        (mx, lax.rem(my + 1, ny)),
        (mx, lax.rem(my + ny - 1, ny)),
    )
    against = (toward[1], toward[0], toward[3], toward[2])

    barrier = pltpu.get_barrier_semaphore()
    for device in toward:
        pl.semaphore_signal(barrier, inc=1, device_id=device, device_id_type=pl.DeviceIdType.MESH)

    held = (
        pos_ref, vel_ref, spec_ref, cen_ref, nei_ref, cnt_ref, gl_ref, ml_ref,
        wr_ref, ce_ref, ne_ref, pw_ref, mi_ref, mo_ref, fw_ref, eh_ref,
    )
    given = (
        pos_in, vel_in, spec_in, cen_in, nei_in, cnt_in, gl_in, ml_in,
        wr_in, ce_in, ne_in, pw_in, mi_in, mo_in, fw_in, eh_in,
    )
    loads = [pltpu.make_async_copy(given[k], held[k], lsem.at[k]) for k in range(16)]
    first = (0, 2, 6)
    second = (3, 4, 5)
    later = (1, 7, 8, 9, 10, 11, 12, 13, 14, 15)
    for k in first + second + later:
        loads[k].start()

    def copy(turn, face, source, target, device):
        return pltpu.make_async_remote_copy(
            src_ref=source.at[face],
            dst_ref=target.at[face],
            send_sem=ssem.at[turn, face],
            recv_sem=rsem.at[turn, face],
            device_id=device,
            device_id_type=pl.DeviceIdType.MESH,
        )

    def send(turn, source, target, where):
        copies = [copy(turn, face, source, target, where[face]) for face in (2, 3, 0, 1)]
        for one in copies:
            one.start()
        return copies

    stk[...] = jnp.zeros_like(stk)
    for k in first:
        loads[k].wait()
    for m in range(3):
        stk[m:m + 1, :] = pos_ref[0, m]
    stk[3:4, :] = spec_ref[0].astype(F32)
    own = stk[...]
    atom_id = lax.broadcasted_iota(jnp.int32, (ATOMS, GHOST), 0)
    for face in range(4):
        ghot[:, face * GHOST:(face + 1) * GHOST] = jnp.where(
            atom_id == gl_ref[0, 0, face:face + 1, :], 1.0, 0.0
        ).astype(BF16)
    lent_rows = exact_rows(own, ghot[...], mm)
    row8 = lax.broadcasted_iota(jnp.int32, (8, GHOST), 0)
    frame = (
        jnp.where(row8 == 0, -1.0, 0.0),
        jnp.where(row8 == 0, 1.0, 0.0),
        jnp.where(row8 == 1, -1.0, 0.0),
        jnp.where(row8 == 1, 1.0, 0.0),
    )
    for face in range(4):
        s1[face] = lent_rows[:, face * GHOST:(face + 1) * GHOST] + frame[face]
    pl.semaphore_wait(barrier, 4)
    sent = send(0, s1, r1, toward)

    for k in second:
        loads[k].wait()
    center = cen_ref[0]
    neighbor = nei_ref[0]
    edge_id = lax.broadcasted_iota(jnp.int32, (1, EDGES), 1)
    used = edge_id < cnt_ref[0, 0]
    mask = jnp.where(used, 1.0, 0.0)
    atom_edge = lax.broadcasted_iota(jnp.int32, (ATOMS, EDGES), 0)
    chot = jnp.where(atom_edge == center, 1.0, 0.0)
    nhot = jnp.where(atom_edge == neighbor, 1.0, 0.0)
    dhot[...] = (nhot - chot).astype(BF16)
    at_center = exact_rows(own, chot.astype(BF16), mm)
    at_neighbor = exact_rows(own, nhot.astype(BF16), mm)
    ghost_edge = lax.broadcasted_iota(jnp.int32, (4 * GHOST, EDGES), 0) + ATOMS
    nghost[...] = jnp.where(ghost_edge == neighbor, 1.0, 0.0).astype(BF16)

    row_id = jnp.where(used, center, -1).astype(F32)
    column = jnp.transpose(
        jnp.broadcast_to(jnp.where(used, center, -2).astype(F32), (128, EDGES))
    )
    neighbor_id = neighbor.astype(F32)
    ghost_id = gl_ref[0, 0].astype(F32)
    for part in range(4):
        rows = slice(part * 128, part * 128 + 128)
        col = jnp.concatenate([column[rows]] * 4, axis=1)
        k0[rows, :] = jnp.where(col == row_id, ENV_SCALE, 0.0).astype(BF16)
        lmat[rows, :] = jnp.where(col == neighbor_id, ENV_SCALE, 0.0).astype(BF16)
        for face in range(4):
            mmat[rows, face * GHOST:(face + 1) * GHOST] = jnp.where(
                column[rows] == ghost_id[face:face + 1], ENV_SCALE, 0.0
            ).astype(BF16)

    for k in later:
        loads[k].wait()
    wbase[...] = jnp.zeros_like(wbase)
    wbase[0:8, :] = wr_ref[...]
    wbase[8:13, :] = ce_ref[...]
    wbase[16:21, :] = ne_ref[...]
    first_h, first_m, first_l = split3f(wbase[...])
    first_w = jnp.transpose(
        jnp.concatenate(
            [first_h, first_m, first_l, first_h[0:8], first_m[0:8], first_h[0:8], jnp.zeros((32, CH), F32)],
            axis=0,
        )
    ).astype(BF16)
    radial_w = wide4(wr_ref[...])
    product_f = [wide6_t(pw_ref[layer]) for layer in range(2)]
    product_b = [tall2(pw_ref[layer]) for layer in range(2)]
    mixin_f = [tall3(mi_ref[layer]) for layer in range(2)]
    mixin_b = [wide4_t(mi_ref[layer]) for layer in range(2)]
    mixout_f = wide6_t(mo_ref[0])
    mixout_b = wide4(mo_ref[0])
    feature_f = wide6_t(fw_ref[...])
    feature_b = wide4(fw_ref[...])
    head = eh_ref[...]
    square = lax.broadcasted_iota(jnp.int32, (CH, CH), 0) == lax.broadcasted_iota(jnp.int32, (CH, CH), 1)
    head_col = jnp.sum(jnp.where(square, head, 0.0), axis=1, keepdims=True)
    turned = jnp.sum(mo_ref[1] * head, axis=1, keepdims=True)

    for face in range(4):
        copy(0, face, s1, r1, toward[face]).wait_recv()
    ghosts = jnp.concatenate([r1[face] for face in range(4)], axis=1)
    at_neighbor = at_neighbor + exact_rows(ghosts, nghost[...], mm)
    sep = at_neighbor - at_center
    sx, sy, sz = sep[0:1], sep[1:2], sep[2:3]
    length = jnp.sqrt(sx * sx + sy * sy + sz * sz + SOFTENING)
    inv = 1.0 / length
    ux, uy, uz = sx * inv, sy * inv, sz * inv
    yrow[...] = jnp.zeros_like(yrow)
    yrow[0:1, :] = ROOT_THREE * ux
    yrow[1:2, :] = ROOT_THREE * uy
    yrow[2:3, :] = ROOT_THREE * uz
    yrow[8:9, :] = ROOT_FIFTEEN * ux * uy
    yrow[9:10, :] = ROOT_FIFTEEN * uy * uz
    yrow[10:11, :] = 0.5 * ROOT_FIVE * (3.0 * uz * uz - 1.0)
    yrow[11:12, :] = ROOT_FIFTEEN * ux * uz
    yrow[12:13, :] = 0.5 * ROOT_FIFTEEN * (ux * ux - uy * uy)
    y1h, y1m, y1l = split3f(yrow[0:8, :])
    y2h, y2m, y2l = split3f(yrow[8:16, :])
    zero8 = jnp.zeros((8, EDGES), F32)
    left = jnp.concatenate(
        [y1h, y1h, y1h, y1m, y1m, y1l, y2h, y2h, y2h, y2m, y2m, y2l] + [zero8] * 4, axis=0
    )
    left_t = jnp.transpose(left).astype(BF16)
    right1 = jnp.concatenate([y1h, y1m, y1l, y1h, y1m, y1h] + [zero8] * 10, axis=0).astype(BF16)
    right2 = jnp.concatenate(
        [zero8] * 6 + [y2h, y2m, y2l, y2h, y2m, y2h] + [zero8] * 4, axis=0
    ).astype(BF16)
    for part in range(4):
        rows = slice(part * 128, part * 128 + 128)
        same = k0[rows, :].astype(F32)
        k1h[rows, :], k1l[rows, :] = split2(same * mm(left_t[rows], right1))
        k2h[rows, :], k2l[rows, :] = split2(same * mm(left_t[rows], right2))

    basis_at = (BASIS_REACH / 7.0) * lax.broadcasted_iota(jnp.int32, (8, EDGES), 0).astype(F32)
    apart = (length - basis_at) * (1.0 / BASIS_WIDTH)
    radial = jnp.exp(-(apart * apart))
    level = lax.broadcasted_iota(jnp.int32, (8, EDGES), 0).astype(F32)
    hot_c = jnp.where(level == at_center[3:4], 1.0, 0.0)
    hot_n = jnp.where(level == at_neighbor[3:4], 1.0, 0.0)
    rad_h, rad_m, rad_l = split3f(radial)
    first_x = jnp.concatenate(
        [rad_h, hot_c, hot_n] * 3 + [rad_m, rad_m, rad_l] + [zero8] * 4, axis=0
    ).astype(BF16)
    before = mm(first_w, first_x)
    first_gate = 0.5 * (1.0 + jnp.tanh(0.5 * before))
    initial = before * first_gate

    def env(values, degree):
        three = jnp.concatenate(split3(values), axis=0)
        out = mm(three, (k0, k1h, k2h)[degree][...])
        small = out[CH:2 * CH] + out[2 * CH:]
        if degree > 0:
            low = mm(three[0:2 * CH], (None, k1l, k2l)[degree][...])
            small = small + low[0:CH] + low[CH:]
        return out[0:CH] + small

    def layer_front(hidden, layer):
        coupled = mm(product_f[layer], stack6(hidden))
        blocks = [coupled[d * CH:(d + 1) * CH] for d in range(3)]
        environ = [env(blocks[d], d) for d in range(3)]
        joined = jnp.concatenate([hidden] + [blocks[d] * environ[d] for d in range(3)], axis=0)
        inner = mm_tall3(mixin_f[layer], joined)
        gate = 0.5 * (1.0 + jnp.tanh(0.5 * inner))
        return blocks, environ, inner, gate

    def layer_back(grad_inner, grad_out, blocks, environ, layer):
        grad_joined = mm(mixin_b[layer], stack4(grad_inner))
        pulls = [grad_joined[(d + 1) * CH:(d + 2) * CH] for d in range(3)]
        scaled = [pulls[d] * blocks[d] for d in range(3)]
        grad_coupled = jnp.concatenate(
            [pulls[d] * environ[d] + env(scaled[d], d) for d in range(3)], axis=0
        )
        grad_hidden = grad_out + grad_joined[0:CH] + mm_tall2(product_b[layer], grad_coupled)
        return grad_hidden, scaled

    def pair_sums(blocks, scaled, psum):
        for d in (1, 2):
            bh, bl = split2(blocks[d])
            ah, al = split2(scaled[d])
            lhs = jnp.concatenate([bh, bl, ah, al], axis=0)
            rhs = jnp.concatenate([ah, ah, bh, bh], axis=0)
            lhs2 = jnp.concatenate([bh, ah], axis=0)
            rhs2 = jnp.concatenate([al, bl], axis=0)
            psum[d - 1] = mm_tn(lhs, rhs) + mm_tn(lhs2, rhs2)

    blocks0, environ0, inner0, gate0 = layer_front(initial, 0)
    hidden = initial + mm(mixout_f, stack6(inner0 * gate0))

    carried = mm(feature_f, stack6(hidden))
    lent = many_rows(carried, mmat[...], mm)
    for face in range(4):
        s2[face] = lent[:, face * GHOST:(face + 1) * GHOST]
    sent += send(1, s2, r2, toward)
    combined = hidden + many_rows(carried, lmat[...], mm)
    for face in range(4):
        copy(1, face, s2, r2, toward[face]).wait_recv()
    borrowed = jnp.concatenate([r2[face] for face in range(4)], axis=1)
    combined = combined + many_rows(borrowed, nghost[...], mm)

    blocks1, environ1, inner1, gate1 = layer_front(combined, 1)
    grad_inner = turned * mask * (gate1 * (1.0 + inner1 * (1.0 - gate1)))
    grad_combined, scaled1 = layer_back(grad_inner, head_col * mask, blocks1, environ1, 1)
    back = many_rows(grad_combined, nghost[...], mm_nt)
    for face in range(4):
        s3[face] = back[:, face * GHOST:(face + 1) * GHOST]
    sent += send(2, s3, r3, against)
    grad_carried = many_rows(grad_combined, lmat[...], mm_nt)
    pair_sums(blocks1, scaled1, psum2)
    for face in range(4):
        copy(2, face, s3, r3, against[face]).wait_recv()
    returned = jnp.concatenate([r3[face] for face in range(4)], axis=1)
    grad_carried = grad_carried + many_rows(returned, mmat[...], mm_nt)
    grad_hidden = grad_combined + mm(feature_b, stack4(grad_carried))

    grad_inner = mm(mixout_b, stack4(grad_hidden)) * (gate0 * (1.0 + inner0 * (1.0 - gate0)))
    grad_initial, scaled0 = layer_back(grad_inner, grad_hidden, blocks0, environ0, 0)
    pair_sums(blocks0, scaled0, psum1)
    grad_before = grad_initial * (first_gate * (1.0 + before * (1.0 - first_gate)))
    grad_radial = mm(radial_w, stack4(grad_before))
    grad_length = jnp.sum(grad_radial * radial * apart, axis=0, keepdims=True) * (-2.0 / BASIS_WIDTH)

    grad_y = []
    for d, (yh, yl) in enumerate(((y1h, y1m), (y2h, y2m))):
        rows = jnp.concatenate([yh, yl], axis=0).astype(BF16)
        total = None
        for part in range(4):
            span = slice(part * 128, part * 128 + 128)
            pair = (psum1[d, span, :] + psum2[d, span, :]) * k0[span, :].astype(F32)
            ph, pn = split2(pair)
            one = mm(rows[:, span], ph)
            one = one[0:8] + one[8:16] + mm(rows[:, span], pn)[0:8]
            total = one if total is None else total + one
        grad_y.append(total)
    g1x, g1y, g1z = (grad_y[0][m:m + 1] for m in range(3))
    g20, g21, g22, g23, g24 = (grad_y[1][m:m + 1] for m in range(5))
    dux = ROOT_THREE * g1x + ROOT_FIFTEEN * (uy * g20 + uz * g23 + ux * g24)
    duy = ROOT_THREE * g1y + ROOT_FIFTEEN * (ux * g20 + uz * g21 - uy * g24)
    duz = ROOT_THREE * g1z + ROOT_FIFTEEN * (uy * g21 + ux * g23) + (3.0 * ROOT_FIVE) * uz * g22
    along = grad_length - inv * (dux * ux + duy * uy + duz * uz)
    grow[...] = jnp.zeros_like(grow)
    grow[0:1, :] = inv * dux + along * ux
    grow[1:2, :] = inv * duy + along * uy
    grow[2:3, :] = inv * duz + along * uz
    grad_sep = grow[...]

    back = exact_rows(grad_sep, nghost[...], mm_nt)
    for face in range(4):
        s4[face] = back[:, face * GHOST:(face + 1) * GHOST]
    sent += send(3, s4, r4, against)
    grad_local = exact_rows(grad_sep, dhot[...], mm_nt)
    species = spec_ref[0]
    inverse = jnp.zeros((1, ATOMS), F32)
    for kind, value in enumerate(INVERSE_MASS):
        inverse = jnp.where(species == kind, value, inverse)
    mig_atom = lax.broadcasted_iota(jnp.int32, (ATOMS, MIG), 0)
    moves = jnp.concatenate(
        [jnp.where(mig_atom == ml_ref[0, 0, face:face + 1, :], 1.0, 0.0) for face in range(4)]
        + [jnp.zeros((ATOMS, 4 * MIG), F32)], axis=1
    ).astype(BF16)
    stays = 1.0 - mm_nt(jnp.ones((16, 8 * MIG), BF16), moves)[0:8]
    for face in range(4):
        copy(3, face, s4, r4, against[face]).wait_recv()
    returned = jnp.concatenate([r4[face] for face in range(4)], axis=1)
    grad_local = grad_local + exact_rows(returned, ghot[...], mm_nt)
    forces = -grad_local
    for m in range(3):
        f_out[0, m] = forces[m:m + 1]
        stk[m:m + 1, :] = vel_ref[0, m]
    velocity = stk[...] + STEP_TIME * forces * inverse
    position = own + STEP_TIME * velocity

    f_store = pltpu.make_async_copy(f_out, home.at[:, 0:3], osem.at[0])
    f_store.start()

    moved_p = exact_rows(position, moves, mm)
    moved_v = exact_rows(velocity, moves, mm)
    lane = lax.broadcasted_iota(jnp.int32, (8, 8 * MIG), 1) // MIG
    row = lax.broadcasted_iota(jnp.int32, (8, 8 * MIG), 0)
    shift = jnp.where((row == 0) & (lane == 0), -1.0, 0.0) + jnp.where((row == 0) & (lane == 1), 1.0, 0.0)
    shift = shift + jnp.where((row == 1) & (lane == 2), -1.0, 0.0) + jnp.where((row == 1) & (lane == 3), 1.0, 0.0)
    leaving = jnp.concatenate([moved_p + shift, moved_v], axis=0)
    for face in range(4):
        s5[face] = jnp.where(lax.broadcasted_iota(jnp.int32, (16, 8 * MIG), 1) // MIG == face, leaving, 0.0)
    sent += send(4, s5, r5, toward)
    for face in range(4):
        copy(4, face, s5, r5, toward[face]).wait_recv()
    landed = r5[0] + r5[1] + r5[2] + r5[3]
    position = position * stays + exact_rows(landed[0:8], moves, mm_nt)
    velocity = velocity * stays + exact_rows(landed[8:16], moves, mm_nt)
    for m in range(3):
        p_out[0, m] = position[m:m + 1]
        v_out[0, m] = velocity[m:m + 1]
    p_store = pltpu.make_async_copy(p_out, home.at[:, 3:6], osem.at[1])
    v_store = pltpu.make_async_copy(v_out, home.at[:, 6:9], osem.at[2])
    p_store.start()
    v_store.start()
    for one in sent:
        one.wait_send()
    for one in (f_store, p_store, v_store):
        one.wait()


def solution(mesh):
    nx, ny = mesh.shape["gx"], mesh.shape["gy"]
    placed = (
        P("gx", "gy", None, None),
        P("gx", "gy", None, None),
        P("gx", "gy", None),
        P("gx", "gy", None),
        P("gx", "gy", None),
        P("gx", "gy"),
        P("gx", "gy", None, None),
        P("gx", "gy", None, None),
        P(),
        P(),
        P(),
        P(),
        P(),
        P(),
        P(),
        P(),
    )

    def step(*operands):
        operands = list(operands)
        operands[0] = operands[0].transpose(0, 2, 1, 3)
        operands[1] = operands[1].transpose(0, 2, 1, 3)
        operands[12] = operands[12].transpose(0, 2, 1)
        operands[15] = operands[15].reshape(1, CH)
        vmem = pl.BlockSpec(memory_space=pltpu.VMEM)
        specs = [pl.BlockSpec(memory_space=pltpu.HBM)] * 16
        held = [pltpu.VMEM(one.shape, one.dtype) for one in operands]
        held[5] = pltpu.SMEM((1, 1), jnp.int32)
        big = pltpu.VMEM((EDGES, EDGES), BF16)

        def boxes(rows, width=GHOST):
            return [pltpu.VMEM((4, rows, width), F32)] * 2

        out = jax.ShapeDtypeStruct((1, 3, 1, ATOMS), F32)
        results = pl.pallas_call(
            functools.partial(kernel, nx, ny),
            out_shape=[jax.ShapeDtypeStruct((1, 9, 1, ATOMS), F32)],
            in_specs=specs,
            out_specs=[pl.BlockSpec(memory_space=pltpu.HBM)],
            scratch_shapes=[
                *[pltpu.VMEM((1, 3, 1, ATOMS), F32)] * 3,
                *held,
                pltpu.VMEM((8, ATOMS), F32),
                pltpu.VMEM((24, CH), F32),
                big, big, big, big, big, big, big, big,
                pltpu.VMEM((ATOMS, EDGES), BF16),
                pltpu.VMEM((ATOMS, EDGES), BF16),
                pltpu.VMEM((2, EDGES, EDGES), F32),
                pltpu.VMEM((2, EDGES, EDGES), F32),
                pltpu.VMEM((16, EDGES), F32),
                pltpu.VMEM((8, EDGES), F32),
                *boxes(8), *boxes(CH), *boxes(CH), *boxes(8), *boxes(16, 8 * MIG),
                pltpu.SemaphoreType.DMA((5, 4)),
                pltpu.SemaphoreType.DMA((5, 4)),
                pltpu.SemaphoreType.DMA((16,)),
                pltpu.SemaphoreType.DMA((3,)),
            ],
            compiler_params=pltpu.CompilerParams(
                collective_id=0, has_side_effects=True, vmem_limit_bytes=60 * 1024 * 1024
            ),
        )(*operands)
        whole = results[0].transpose(0, 2, 1, 3)
        return whole[:, :, 0:3], whole[:, :, 3:6], whole[:, :, 6:9]

    face = P("gx", "gy", None, None)
    return jax.shard_map(
        step, mesh=mesh, in_specs=placed, out_specs=(face, face, face), check_vma=False
    )
```

```python
import functools

import jax
import jax.numpy as jnp
from jax import lax
from jax.experimental import pallas as pl
from jax.experimental.pallas import tpu as pltpu
from jax.sharding import PartitionSpec as P

F32 = jnp.float32
BF16 = jnp.bfloat16
ENV_SCALE = 0.5
SOFTENING = 0.04
STEP_TIME = 0.1
BASIS_WIDTH = 0.4
BASIS_REACH = 2.5
INVERSE_MASS = (0.992063, 0.083257, 0.071393, 0.062504, 0.031192)
ROOT_THREE = 3.0**0.5
ROOT_FIVE = 5.0**0.5
ROOT_FIFTEEN = 15.0**0.5
ATOMS = 256
GHOST = 128
EDGES = 512
CH = 64
MIG = 16


def split2(x):
    hi = x.astype(BF16)
    return hi, (x - hi.astype(F32)).astype(BF16)


def split2f(x):
    hi = x.astype(BF16).astype(F32)
    return hi, x - hi


def split3f(x):
    hi = x.astype(BF16).astype(F32)
    rest = x - hi
    mid = rest.astype(BF16).astype(F32)
    return hi, mid, rest - mid


def mm(a, b):
    return lax.dot_general(a, b, (((1,), (0,)), ((), ())), preferred_element_type=F32)


def mm_nt(a, b):
    return lax.dot_general(a, b, (((1,), (1,)), ((), ())), preferred_element_type=F32)


def mm_tn(a, b):
    return lax.dot_general(a, b, (((0,), (0,)), ((), ())), preferred_element_type=F32)


def stack4(x):
    hi, lo = split2(x)
    return jnp.concatenate([hi, hi, lo, lo], axis=0)


def split3(x):
    hi = x.astype(BF16)
    rest = x - hi.astype(F32)
    mid = rest.astype(BF16)
    return hi, mid, (rest - mid.astype(F32)).astype(BF16)


def stack6(x):
    hi, mid, lo = split3(x)
    return jnp.concatenate([hi, mid, lo, hi, mid, hi], axis=0)


def exact_rows(x, hot, product):
    hi, mid, lo = split3f(x)
    parts = jnp.concatenate([hi, mid, lo, jnp.zeros_like(lo)], axis=0).astype(BF16)
    out = product(parts, hot)
    return out[0:8] + out[8:16] + out[16:24]


def many_rows(x, hot, product):
    rows = x.shape[0]
    out = product(jnp.concatenate(split3(x), axis=0), hot)
    return out[0:rows] + (out[rows:2 * rows] + out[2 * rows:])


def wide4(w):
    hi, lo = split2f(w)
    return jnp.concatenate([hi, lo, hi, lo], axis=1).astype(BF16)


def wide4_t(w):
    hi, lo = split2f(w)
    return jnp.transpose(jnp.concatenate([hi, lo, hi, lo], axis=0)).astype(BF16)


def wide6_t(w):
    hi, mid, lo = split3f(w)
    return jnp.transpose(jnp.concatenate([hi, hi, hi, mid, mid, lo], axis=0)).astype(BF16)


def tall2(w):
    hi, lo = split2f(w)
    return jnp.concatenate([hi, lo], axis=0).astype(BF16)


def tall3(w):
    return jnp.concatenate(split3f(w), axis=0).astype(BF16)


def mm_tall2(w2, x):
    rows = w2.shape[0] // 2
    hi, lo = split2(x)
    out = mm(w2, hi)
    small = mm(w2, lo)
    return out[0:rows] + (out[rows:] + small[0:rows] + small[rows:])


def mm_tall3(w3, x):
    rows = w3.shape[0] // 3
    hi, mid, lo = split3(x)
    first = mm(w3, hi)
    second = mm(w3[0:2 * rows], mid)
    third = mm(w3[0:rows], lo)
    return first[0:rows] + (
        first[rows:2 * rows] + second[0:rows] + (first[2 * rows:] + second[rows:] + third)
    )


def kernel(
    nx, ny,
    pos_in, vel_in, spec_in, cen_in, nei_in, cnt_in, gl_in, ml_in,
    wr_in, ce_in, ne_in, pw_in, mi_in, mo_in, fw_in, eh_in,
    home,
    f_out, p_out, v_out,
    pos_ref, vel_ref, spec_ref, cen_ref, nei_ref, cnt_ref, gl_ref, ml_ref,
    wr_ref, ce_ref, ne_ref, pw_ref, mi_ref, mo_ref, fw_ref, eh_ref,
    stk, wbase, k0, k1h, k1l, k2h, k2l, lmat, mmat, nghost, ghot, dhot, psum1, psum2, yrow, grow,
    s1, r1, s2, r2, s3, r3, s4, r4, s5, r5, s6, r6, r7, later_hot, mig_hot, edge_mig, ssem, rsem, lsem, osem,
):
    mx = lax.axis_index("gx")
    my = lax.axis_index("gy")
    toward = (
        (lax.rem(mx + 1, nx), my),
        (lax.rem(mx + nx - 1, nx), my),
        (mx, lax.rem(my + 1, ny)),
        (mx, lax.rem(my + ny - 1, ny)),
    )
    against = (toward[1], toward[0], toward[3], toward[2])
    corners = ((0, 2), (0, 3), (1, 2), (1, 3))
    corner = [(toward[fx][0], toward[fy][1]) for fx, fy in corners]
    straight = (
        (lax.rem(mx + 2, nx), my),
        (lax.rem(mx + nx - 2, nx), my),
        (mx, lax.rem(my + 2, ny)),
        (mx, lax.rem(my + ny - 2, ny)),
    )

    barrier = pltpu.get_barrier_semaphore()
    for device in toward:
        pl.semaphore_signal(barrier, inc=1, device_id=device, device_id_type=pl.DeviceIdType.MESH)

    held = (
        pos_ref, vel_ref, spec_ref, cen_ref, nei_ref, cnt_ref, gl_ref, ml_ref,
        wr_ref, ce_ref, ne_ref, pw_ref, mi_ref, mo_ref, fw_ref, eh_ref,
    )
    given = (
        pos_in, vel_in, spec_in, cen_in, nei_in, cnt_in, gl_in, ml_in,
        wr_in, ce_in, ne_in, pw_in, mi_in, mo_in, fw_in, eh_in,
    )
    loads = [pltpu.make_async_copy(given[k], held[k], lsem.at[k]) for k in range(16)]
    first = (0, 2, 6)
    second = (1, 7, 3, 4, 5)
    later = (8, 9, 10, 11, 12, 13, 14, 15)
    for k in first + second + later:
        loads[k].start()

    def copy(turn, face, source, target, device):
        return pltpu.make_async_remote_copy(
            src_ref=source.at[face],
            dst_ref=target.at[face],
            send_sem=ssem.at[turn, face],
            recv_sem=rsem.at[turn, face],
            device_id=device,
            device_id_type=pl.DeviceIdType.MESH,
        )

    def send(turn, source, target, where):
        copies = [copy(turn, face, source, target, where[face]) for face in (2, 3, 0, 1)]
        for one in copies:
            one.start()
        return copies

    stk[...] = jnp.zeros_like(stk)
    for k in first:
        loads[k].wait()
    for m in range(3):
        stk[m:m + 1, :] = pos_ref[0, m]
    stk[3:4, :] = spec_ref[0].astype(F32)
    own = stk[...]
    atom_id = lax.broadcasted_iota(jnp.int32, (ATOMS, GHOST), 0)
    for face in range(4):
        ghot[:, face * GHOST:(face + 1) * GHOST] = jnp.where(
            atom_id == gl_ref[0, 0, face:face + 1, :], 1.0, 0.0
        ).astype(BF16)
    lent_rows = exact_rows(own, ghot[...], mm)
    row8 = lax.broadcasted_iota(jnp.int32, (8, GHOST), 0)
    frame = (
        jnp.where(row8 == 0, -1.0, 0.0),
        jnp.where(row8 == 0, 1.0, 0.0),
        jnp.where(row8 == 1, -1.0, 0.0),
        jnp.where(row8 == 1, 1.0, 0.0),
    )
    for face in range(4):
        s1[face] = lent_rows[:, face * GHOST:(face + 1) * GHOST] + frame[face]
    pl.semaphore_wait(barrier, 4)
    sent = send(0, s1, r1, toward)

    for k in second:
        loads[k].wait()
    ghost_id = gl_ref[0, 0].astype(F32)
    mig_lane = lax.broadcasted_iota(jnp.int32, (1, GHOST), 1) // MIG
    mig_id = jnp.concatenate(
        [ml_ref[0, 0, face:face + 1, :].astype(F32) for face in range(4)]
        + [jnp.full((1, GHOST - 4 * MIG), -1.0, F32)], axis=1
    )
    atom_row = atom_id.astype(F32)
    moves = jnp.where(atom_row == mig_id, 1.0, 0.0).astype(BF16)
    mig_hot[...] = moves
    stk[...] = jnp.zeros_like(stk)
    for m in range(3):
        stk[m:m + 1, :] = vel_ref[0, m]
    speed = stk[...]
    lane8 = lax.broadcasted_iota(jnp.int32, (8, GHOST), 1) // MIG
    moved_p = exact_rows(own, moves, mm)
    moved_v = exact_rows(speed, moves, mm)
    for face in range(4):
        s5[face, 0:8, :] = jnp.where(lane8 == face, moved_p + frame[face], 0.0)
        s5[face, 8:16, :] = jnp.where(lane8 == face, moved_v, 0.0)
        s5[face, 16:17, :] = jnp.where(mig_lane == face, mig_id, -1.0)
        s5[face, 17:21, :] = ghost_id
        s5[face, 21:24, :] = jnp.zeros((3, GHOST), F32)
    sent += send(4, s5, r5, toward)

    center = cen_ref[0]
    neighbor = nei_ref[0]
    edge_id = lax.broadcasted_iota(jnp.int32, (1, EDGES), 1)
    used = edge_id < cnt_ref[0, 0]
    mask = jnp.where(used, 1.0, 0.0)
    atom_edge = lax.broadcasted_iota(jnp.int32, (ATOMS, EDGES), 0)
    chot = jnp.where(atom_edge == center, 1.0, 0.0)
    nhot = jnp.where(atom_edge == neighbor, 1.0, 0.0)
    dhot[...] = (nhot - chot).astype(BF16)
    edge_mig[...] = mm_tn(dhot[...], moves).astype(BF16)
    at_center = exact_rows(own, chot.astype(BF16), mm)
    at_neighbor = exact_rows(own, nhot.astype(BF16), mm)
    ghost_edge = lax.broadcasted_iota(jnp.int32, (4 * GHOST, EDGES), 0) + ATOMS
    nghost[...] = jnp.where(ghost_edge == neighbor, 1.0, 0.0).astype(BF16)

    row_id = jnp.where(used, center, -1).astype(F32)
    column = jnp.transpose(
        jnp.broadcast_to(jnp.where(used, center, -2).astype(F32), (128, EDGES))
    )
    neighbor_id = neighbor.astype(F32)
    for part in range(4):
        rows = slice(part * 128, part * 128 + 128)
        col = jnp.concatenate([column[rows]] * 4, axis=1)
        k0[rows, :] = jnp.where(col == row_id, ENV_SCALE, 0.0).astype(BF16)
        lmat[rows, :] = jnp.where(col == neighbor_id, ENV_SCALE, 0.0).astype(BF16)
        for face in range(4):
            mmat[rows, face * GHOST:(face + 1) * GHOST] = jnp.where(
                column[rows] == ghost_id[face:face + 1], ENV_SCALE, 0.0
            ).astype(BF16)

    for k in later:
        loads[k].wait()
    wbase[...] = jnp.zeros_like(wbase)
    wbase[0:8, :] = wr_ref[...]
    wbase[8:13, :] = ce_ref[...]
    wbase[16:21, :] = ne_ref[...]
    first_h, first_m, first_l = split3f(wbase[...])
    first_w = jnp.transpose(
        jnp.concatenate(
            [first_h, first_m, first_l, first_h[0:8], first_m[0:8], first_h[0:8], jnp.zeros((32, CH), F32)],
            axis=0,
        )
    ).astype(BF16)
    radial_w = wide4(wr_ref[...])
    product_f = [wide6_t(pw_ref[layer]) for layer in range(2)]
    product_b = [tall2(pw_ref[layer]) for layer in range(2)]
    mixin_f = [tall3(mi_ref[layer]) for layer in range(2)]
    mixin_b = [wide4_t(mi_ref[layer]) for layer in range(2)]
    mixout_f = wide6_t(mo_ref[0])
    mixout_b = wide4(mo_ref[0])
    feature_f = wide6_t(fw_ref[...])
    feature_b = wide4(fw_ref[...])
    head = eh_ref[...]
    square = lax.broadcasted_iota(jnp.int32, (CH, CH), 0) == lax.broadcasted_iota(jnp.int32, (CH, CH), 1)
    head_col = jnp.sum(jnp.where(square, head, 0.0), axis=1, keepdims=True)
    turned = jnp.sum(mo_ref[1] * head, axis=1, keepdims=True)

    for face in range(4):
        copy(0, face, s1, r1, toward[face]).wait_recv()
    ghosts = jnp.concatenate([r1[face] for face in range(4)], axis=1)
    at_neighbor = at_neighbor + exact_rows(ghosts, nghost[...], mm)
    sep = at_neighbor - at_center
    sx, sy, sz = sep[0:1], sep[1:2], sep[2:3]
    length = jnp.sqrt(sx * sx + sy * sy + sz * sz + SOFTENING)
    inv = 1.0 / length
    ux, uy, uz = sx * inv, sy * inv, sz * inv
    yrow[...] = jnp.zeros_like(yrow)
    yrow[0:1, :] = ROOT_THREE * ux
    yrow[1:2, :] = ROOT_THREE * uy
    yrow[2:3, :] = ROOT_THREE * uz
    yrow[8:9, :] = ROOT_FIFTEEN * ux * uy
    yrow[9:10, :] = ROOT_FIFTEEN * uy * uz
    yrow[10:11, :] = 0.5 * ROOT_FIVE * (3.0 * uz * uz - 1.0)
    yrow[11:12, :] = ROOT_FIFTEEN * ux * uz
    yrow[12:13, :] = 0.5 * ROOT_FIFTEEN * (ux * ux - uy * uy)
    y1h, y1m, y1l = split3f(yrow[0:8, :])
    y2h, y2m, y2l = split3f(yrow[8:16, :])
    zero8 = jnp.zeros((8, EDGES), F32)
    left = jnp.concatenate(
        [y1h, y1h, y1h, y1m, y1m, y1l, y2h, y2h, y2h, y2m, y2m, y2l] + [zero8] * 4, axis=0
    )
    left_t = jnp.transpose(left).astype(BF16)
    right1 = jnp.concatenate([y1h, y1m, y1l, y1h, y1m, y1h] + [zero8] * 10, axis=0).astype(BF16)
    right2 = jnp.concatenate(
        [zero8] * 6 + [y2h, y2m, y2l, y2h, y2m, y2h] + [zero8] * 4, axis=0
    ).astype(BF16)
    for part in range(4):
        rows = slice(part * 128, part * 128 + 128)
        same = k0[rows, :].astype(F32)
        k1h[rows, :], k1l[rows, :] = split2(same * mm(left_t[rows], right1))
        k2h[rows, :], k2l[rows, :] = split2(same * mm(left_t[rows], right2))

    basis_at = (BASIS_REACH / 7.0) * lax.broadcasted_iota(jnp.int32, (8, EDGES), 0).astype(F32)
    apart = (length - basis_at) * (1.0 / BASIS_WIDTH)
    radial = jnp.exp(-(apart * apart))
    level = lax.broadcasted_iota(jnp.int32, (8, EDGES), 0).astype(F32)
    hot_c = jnp.where(level == at_center[3:4], 1.0, 0.0)
    hot_n = jnp.where(level == at_neighbor[3:4], 1.0, 0.0)
    rad_h, rad_m, rad_l = split3f(radial)
    first_x = jnp.concatenate(
        [rad_h, hot_c, hot_n] * 3 + [rad_m, rad_m, rad_l] + [zero8] * 4, axis=0
    ).astype(BF16)
    before = mm(first_w, first_x)
    first_gate = 0.5 * (1.0 + jnp.tanh(0.5 * before))
    initial = before * first_gate

    def env(values, degree):
        three = jnp.concatenate(split3(values), axis=0)
        out = mm(three, (k0, k1h, k2h)[degree][...])
        small = out[CH:2 * CH] + out[2 * CH:]
        if degree > 0:
            low = mm(three[0:2 * CH], (None, k1l, k2l)[degree][...])
            small = small + low[0:CH] + low[CH:]
        return out[0:CH] + small

    def layer_front(hidden, layer):
        coupled = mm(product_f[layer], stack6(hidden))
        blocks = [coupled[d * CH:(d + 1) * CH] for d in range(3)]
        environ = [env(blocks[d], d) for d in range(3)]
        joined = jnp.concatenate([hidden] + [blocks[d] * environ[d] for d in range(3)], axis=0)
        inner = mm_tall3(mixin_f[layer], joined)
        gate = 0.5 * (1.0 + jnp.tanh(0.5 * inner))
        return blocks, environ, inner, gate

    def layer_back(grad_inner, grad_out, blocks, environ, layer):
        grad_joined = mm(mixin_b[layer], stack4(grad_inner))
        pulls = [grad_joined[(d + 1) * CH:(d + 2) * CH] for d in range(3)]
        scaled = [pulls[d] * blocks[d] for d in range(3)]
        grad_coupled = jnp.concatenate(
            [pulls[d] * environ[d] + env(scaled[d], d) for d in range(3)], axis=0
        )
        grad_hidden = grad_out + grad_joined[0:CH] + mm_tall2(product_b[layer], grad_coupled)
        return grad_hidden, scaled

    def pair_sums(blocks, scaled, psum):
        for d in (1, 2):
            bh, bl = split2(blocks[d])
            ah, al = split2(scaled[d])
            lhs = jnp.concatenate([bh, bl, ah, al], axis=0)
            rhs = jnp.concatenate([ah, ah, bh, bh], axis=0)
            lhs2 = jnp.concatenate([bh, ah], axis=0)
            rhs2 = jnp.concatenate([al, bl], axis=0)
            psum[d - 1] = mm_tn(lhs, rhs) + mm_tn(lhs2, rhs2)

    blocks0, environ0, inner0, gate0 = layer_front(initial, 0)
    hidden = initial + mm(mixout_f, stack6(inner0 * gate0))

    carried = mm(feature_f, stack6(hidden))
    lent = many_rows(carried, mmat[...], mm)
    for face in range(4):
        s2[face] = lent[:, face * GHOST:(face + 1) * GHOST]
    sent += send(1, s2, r2, toward)
    combined = hidden + many_rows(carried, lmat[...], mm)
    for face in range(4):
        copy(1, face, s2, r2, toward[face]).wait_recv()
    borrowed = jnp.concatenate([r2[face] for face in range(4)], axis=1)
    combined = combined + many_rows(borrowed, nghost[...], mm)

    blocks1, environ1, inner1, gate1 = layer_front(combined, 1)
    grad_inner = turned * mask * (gate1 * (1.0 + inner1 * (1.0 - gate1)))
    grad_combined, scaled1 = layer_back(grad_inner, head_col * mask, blocks1, environ1, 1)
    back = many_rows(grad_combined, nghost[...], mm_nt)
    for face in range(4):
        s3[face] = back[:, face * GHOST:(face + 1) * GHOST]
    sent += send(2, s3, r3, against)
    grad_carried = many_rows(grad_combined, lmat[...], mm_nt)
    pair_sums(blocks1, scaled1, psum2)
    for face in range(4):
        copy(4, face, s5, r5, toward[face]).wait_recv()
    for face in range(4):
        arrived = jnp.where(atom_row == r5[face, 16:17, :], 1.0, 0.0).astype(BF16)
        for other in range(4):
            lent_there = jnp.where(atom_row == r5[face, 17 + other:18 + other, :], 1.0, 0.0).astype(BF16)
            later_hot[face, other * GHOST:(other + 1) * GHOST, :] = mm_tn(lent_there, arrived).astype(BF16)
    landed_p = r5[0, 0:8] + r5[1, 0:8] + r5[2, 0:8] + r5[3, 0:8]
    landed_v = r5[0, 8:16] + r5[1, 8:16] + r5[2, 8:16] + r5[3, 8:16]
    landed_inverse = jnp.zeros((1, GHOST), F32)
    for kind, value in enumerate(INVERSE_MASS):
        landed_inverse = jnp.where(landed_p[3:4] == float(kind), value, landed_inverse)
    for face in range(4):
        copy(2, face, s3, r3, against[face]).wait_recv()
    returned = jnp.concatenate([r3[face] for face in range(4)], axis=1)
    grad_carried = grad_carried + many_rows(returned, mmat[...], mm_nt)
    grad_hidden = grad_combined + mm(feature_b, stack4(grad_carried))

    grad_inner = mm(mixout_b, stack4(grad_hidden)) * (gate0 * (1.0 + inner0 * (1.0 - gate0)))
    grad_initial, scaled0 = layer_back(grad_inner, grad_hidden, blocks0, environ0, 0)
    pair_sums(blocks0, scaled0, psum1)
    grad_before = grad_initial * (first_gate * (1.0 + before * (1.0 - first_gate)))
    grad_radial = mm(radial_w, stack4(grad_before))
    grad_length = jnp.sum(grad_radial * radial * apart, axis=0, keepdims=True) * (-2.0 / BASIS_WIDTH)

    grad_y = []
    for d, (yh, yl) in enumerate(((y1h, y1m), (y2h, y2m))):
        rows = jnp.concatenate([yh, yl], axis=0).astype(BF16)
        total = None
        for part in range(4):
            span = slice(part * 128, part * 128 + 128)
            pair = (psum1[d, span, :] + psum2[d, span, :]) * k0[span, :].astype(F32)
            ph, pn = split2(pair)
            one = mm(rows[:, span], ph)
            one = one[0:8] + one[8:16] + mm(rows[:, span], pn)[0:8]
            total = one if total is None else total + one
        grad_y.append(total)
    g1x, g1y, g1z = (grad_y[0][m:m + 1] for m in range(3))
    g20, g21, g22, g23, g24 = (grad_y[1][m:m + 1] for m in range(5))
    dux = ROOT_THREE * g1x + ROOT_FIFTEEN * (uy * g20 + uz * g23 + ux * g24)
    duy = ROOT_THREE * g1y + ROOT_FIFTEEN * (ux * g20 + uz * g21 - uy * g24)
    duz = ROOT_THREE * g1z + ROOT_FIFTEEN * (uy * g21 + ux * g23) + (3.0 * ROOT_FIVE) * uz * g22
    along = grad_length - inv * (dux * ux + duy * uy + duz * uz)
    grow[...] = jnp.zeros_like(grow)
    grow[0:1, :] = inv * dux + along * ux
    grow[1:2, :] = inv * duy + along * uy
    grow[2:3, :] = inv * duz + along * uz
    grad_sep = grow[...]

    back = exact_rows(grad_sep, nghost[...], mm_nt)
    leaving = exact_rows(grad_sep, edge_mig[...], mm)
    blocks = [back[:, face * GHOST:(face + 1) * GHOST] for face in range(4)]
    for face in range(4):
        s4[face, 0:8, :] = blocks[face ^ 1]
        s4[face, 8:16, :] = jnp.where(lane8 == face, leaving, 0.0)
    for k, (fx, fy) in enumerate(corners):
        s6[k, 0:8, :] = blocks[fy ^ 1]
        s6[k, 8:16, :] = blocks[fx ^ 1]

    def jump(face):
        return pltpu.make_async_remote_copy(
            src_ref=s4.at[face, pl.ds(0, 8)],
            dst_ref=r7.at[face],
            send_sem=ssem.at[6, face],
            recv_sem=rsem.at[6, face],
            device_id=straight[face],
            device_id_type=pl.DeviceIdType.MESH,
        )

    final = [copy(3, face, s4, r4, toward[face]) for face in (2, 3)]
    final += [copy(5, k, s6, r6, corner[k]) for k in range(4)]
    final += [jump(2), jump(3)]
    final += [copy(3, face, s4, r4, toward[face]) for face in (0, 1)]
    final += [jump(0), jump(1)]
    for one in final:
        one.start()
    sent += final
    grad_local = exact_rows(grad_sep, dhot[...], mm_nt)
    species = spec_ref[0]
    inverse = jnp.zeros((1, ATOMS), F32)
    for kind, value in enumerate(INVERSE_MASS):
        inverse = jnp.where(species == kind, value, inverse)
    moves = mig_hot[...]
    stays = 1.0 - mm_nt(jnp.ones((16, GHOST), BF16), moves)[0:8]
    for one in final:
        one.wait_recv()
    returned = jnp.concatenate([r4[face ^ 1, 0:8, :] for face in range(4)], axis=1)
    grad_local = grad_local + exact_rows(returned, ghot[...], mm_nt)
    grad_landed = r4[0, 8:16, :] + r4[1, 8:16, :] + r4[2, 8:16, :] + r4[3, 8:16, :]
    for face in range(4):
        parts = []
        for other in range(4):
            if other == face:
                parts.append(blocks[face])
            elif other == face ^ 1:
                parts.append(r7[face])
            elif face < 2:
                parts.append(r6[corners.index((face, other ^ 1)), 0:8, :])
            else:
                parts.append(r6[corners.index((other ^ 1, face)), 8:16, :])
        grad_landed = grad_landed + exact_rows(jnp.concatenate(parts, axis=1), later_hot[face], mm)
    velocity = speed - STEP_TIME * grad_local * inverse
    position = own + STEP_TIME * velocity
    landed_v = landed_v - STEP_TIME * grad_landed * landed_inverse
    landed_p = landed_p + STEP_TIME * landed_v
    position = position * stays + exact_rows(landed_p, moves, mm_nt)
    velocity = velocity * stays + exact_rows(landed_v, moves, mm_nt)
    for m in range(3):
        f_out[0, m] = -grad_local[m:m + 1]
        p_out[0, m] = position[m:m + 1]
        v_out[0, m] = velocity[m:m + 1]
    f_store = pltpu.make_async_copy(f_out, home.at[:, 0:3], osem.at[0])
    f_store.start()
    p_store = pltpu.make_async_copy(p_out, home.at[:, 3:6], osem.at[1])
    v_store = pltpu.make_async_copy(v_out, home.at[:, 6:9], osem.at[2])
    p_store.start()
    v_store.start()
    for one in sent:
        one.wait_send()
    for one in (f_store, p_store, v_store):
        one.wait()


def solution(mesh):
    nx, ny = mesh.shape["gx"], mesh.shape["gy"]
    placed = (
        P("gx", "gy", None, None),
        P("gx", "gy", None, None),
        P("gx", "gy", None),
        P("gx", "gy", None),
        P("gx", "gy", None),
        P("gx", "gy"),
        P("gx", "gy", None, None),
        P("gx", "gy", None, None),
        P(),
        P(),
        P(),
        P(),
        P(),
        P(),
        P(),
        P(),
    )

    def step(*operands):
        operands = list(operands)
        operands[0] = operands[0].transpose(0, 2, 1, 3)
        operands[1] = operands[1].transpose(0, 2, 1, 3)
        operands[12] = operands[12].transpose(0, 2, 1)
        operands[15] = operands[15].reshape(1, CH)
        vmem = pl.BlockSpec(memory_space=pltpu.VMEM)
        specs = [pl.BlockSpec(memory_space=pltpu.HBM)] * 16
        held = [pltpu.VMEM(one.shape, one.dtype) for one in operands]
        held[5] = pltpu.SMEM((1, 1), jnp.int32)
        big = pltpu.VMEM((EDGES, EDGES), BF16)

        def boxes(rows, width=GHOST):
            return [pltpu.VMEM((4, rows, width), F32)] * 2

        out = jax.ShapeDtypeStruct((1, 3, 1, ATOMS), F32)
        results = pl.pallas_call(
            functools.partial(kernel, nx, ny),
            out_shape=[jax.ShapeDtypeStruct((1, 9, 1, ATOMS), F32)],
            in_specs=specs,
            out_specs=[pl.BlockSpec(memory_space=pltpu.HBM)],
            scratch_shapes=[
                *[pltpu.VMEM((1, 3, 1, ATOMS), F32)] * 3,
                *held,
                pltpu.VMEM((8, ATOMS), F32),
                pltpu.VMEM((24, CH), F32),
                big, big, big, big, big, big, big, big,
                pltpu.VMEM((ATOMS, EDGES), BF16),
                pltpu.VMEM((ATOMS, EDGES), BF16),
                pltpu.VMEM((2, EDGES, EDGES), F32),
                pltpu.VMEM((2, EDGES, EDGES), F32),
                pltpu.VMEM((16, EDGES), F32),
                pltpu.VMEM((8, EDGES), F32),
                *boxes(8), *boxes(CH), *boxes(CH), *boxes(16), *boxes(24), *boxes(16),
                pltpu.VMEM((4, 8, GHOST), F32),
                pltpu.VMEM((4, EDGES, GHOST), BF16),
                pltpu.VMEM((ATOMS, GHOST), BF16),
                pltpu.VMEM((EDGES, GHOST), BF16),
                pltpu.SemaphoreType.DMA((7, 4)),
                pltpu.SemaphoreType.DMA((7, 4)),
                pltpu.SemaphoreType.DMA((16,)),
                pltpu.SemaphoreType.DMA((3,)),
            ],
            compiler_params=pltpu.CompilerParams(
                collective_id=0, has_side_effects=True, vmem_limit_bytes=60 * 1024 * 1024
            ),
        )(*operands)
        whole = results[0].transpose(0, 2, 1, 3)
        return whole[:, :, 0:3], whole[:, :, 3:6], whole[:, :, 6:9]

    face = P("gx", "gy", None, None)
    return jax.shard_map(
        step, mesh=mesh, in_specs=placed, out_specs=(face, face, face), check_vma=False
    )
```

```python
import functools

import jax
import jax.numpy as jnp
from jax import lax
from jax.experimental import pallas as pl
from jax.experimental.pallas import tpu as pltpu
from jax.sharding import PartitionSpec as P

F32 = jnp.float32
BF16 = jnp.bfloat16
ENV_SCALE = 0.5
SOFTENING = 0.04
STEP_TIME = 0.1
BASIS_WIDTH = 0.4
BASIS_REACH = 2.5
INVERSE_MASS = (0.992063, 0.083257, 0.071393, 0.062504, 0.031192)
ROOT_THREE = 3.0**0.5
ROOT_FIVE = 5.0**0.5
ROOT_FIFTEEN = 15.0**0.5
ATOMS = 256
GHOST = 128
EDGES = 512
CH = 64
MIG = 16


def split2(x):
    hi = x.astype(BF16)
    return hi, (x - hi.astype(F32)).astype(BF16)


def split2f(x):
    hi = x.astype(BF16).astype(F32)
    return hi, x - hi


def split3f(x):
    hi = x.astype(BF16).astype(F32)
    rest = x - hi
    mid = rest.astype(BF16).astype(F32)
    return hi, mid, rest - mid


def mm(a, b):
    return lax.dot_general(a, b, (((1,), (0,)), ((), ())), preferred_element_type=F32)


def mm_nt(a, b):
    return lax.dot_general(a, b, (((1,), (1,)), ((), ())), preferred_element_type=F32)


def mm_tn(a, b):
    return lax.dot_general(a, b, (((0,), (0,)), ((), ())), preferred_element_type=F32)


def stack4(x):
    hi, lo = split2(x)
    return jnp.concatenate([hi, hi, lo, lo], axis=0)


def split3(x):
    hi = x.astype(BF16)
    rest = x - hi.astype(F32)
    mid = rest.astype(BF16)
    return hi, mid, (rest - mid.astype(F32)).astype(BF16)


def stack6(x):
    hi, mid, lo = split3(x)
    return jnp.concatenate([hi, mid, lo, hi, mid, hi], axis=0)


def exact_rows(x, hot, product):
    hi, mid, lo = split3f(x)
    parts = jnp.concatenate([hi, mid, lo, jnp.zeros_like(lo)], axis=0).astype(BF16)
    out = product(parts, hot)
    return out[0:8] + out[8:16] + out[16:24]


def many_rows(x, hot, product):
    rows = x.shape[0]
    out = product(jnp.concatenate(split3(x), axis=0), hot)
    return out[0:rows] + (out[rows:2 * rows] + out[2 * rows:])


def wide4(w):
    hi, lo = split2f(w)
    return jnp.concatenate([hi, lo, hi, lo], axis=1).astype(BF16)


def wide4_t(w):
    hi, lo = split2f(w)
    return jnp.transpose(jnp.concatenate([hi, lo, hi, lo], axis=0)).astype(BF16)


def wide6_t(w):
    hi, mid, lo = split3f(w)
    return jnp.transpose(jnp.concatenate([hi, hi, hi, mid, mid, lo], axis=0)).astype(BF16)


def tall2(w):
    hi, lo = split2f(w)
    return jnp.concatenate([hi, lo], axis=0).astype(BF16)


def tall3(w):
    return jnp.concatenate(split3f(w), axis=0).astype(BF16)


def mm_tall2(w2, x):
    rows = w2.shape[0] // 2
    hi, lo = split2(x)
    out = mm(w2, hi)
    small = mm(w2, lo)
    return out[0:rows] + (out[rows:] + small[0:rows] + small[rows:])


def mm_tall3(w3, x):
    rows = w3.shape[0] // 3
    hi, mid, lo = split3(x)
    first = mm(w3, hi)
    second = mm(w3[0:2 * rows], mid)
    third = mm(w3[0:rows], lo)
    return first[0:rows] + (
        first[rows:2 * rows] + second[0:rows] + (first[2 * rows:] + second[rows:] + third)
    )


def kernel(
    nx, ny,
    pos_in, vel_in, spec_in, cen_in, nei_in, cnt_in, gl_in, ml_in,
    wr_in, ce_in, ne_in, pw_in, mi_in, mo_in, fw_in, eh_in,
    home,
    f_out, p_out, v_out,
    pos_ref, vel_ref, spec_ref, cen_ref, nei_ref, cnt_ref, gl_ref, ml_ref,
    wr_ref, ce_ref, ne_ref, pw_ref, mi_ref, mo_ref, fw_ref, eh_ref,
    stk, wbase, k0, k1h, k1l, k2h, k2l, lmat, mmat, nghost, ghot, dhot, psum1, psum2, yrow, grow,
    s1, r1, s2, r2, s3, r3, s4, r4, s5, r5, s6, r6, r7, later_hot, mig_hot, edge_mig, ssem, rsem, lsem, osem,
):
    mx = lax.axis_index("gx")
    my = lax.axis_index("gy")
    toward = (
        (lax.rem(mx + 1, nx), my),
        (lax.rem(mx + nx - 1, nx), my),
        (mx, lax.rem(my + 1, ny)),
        (mx, lax.rem(my + ny - 1, ny)),
    )
    against = (toward[1], toward[0], toward[3], toward[2])
    corners = ((0, 2), (0, 3), (1, 2), (1, 3))
    corner = [(toward[fx][0], toward[fy][1]) for fx, fy in corners]
    straight = (
        (lax.rem(mx + 2, nx), my),
        (lax.rem(mx + nx - 2, nx), my),
        (mx, lax.rem(my + 2, ny)),
        (mx, lax.rem(my + ny - 2, ny)),
    )

    barrier = pltpu.get_barrier_semaphore()
    for device in toward:
        pl.semaphore_signal(barrier, inc=1, device_id=device, device_id_type=pl.DeviceIdType.MESH)

    held = (
        pos_ref, vel_ref, spec_ref, cen_ref, nei_ref, cnt_ref, gl_ref, ml_ref,
        wr_ref, ce_ref, ne_ref, pw_ref, mi_ref, mo_ref, fw_ref, eh_ref,
    )
    given = (
        pos_in, vel_in, spec_in, cen_in, nei_in, cnt_in, gl_in, ml_in,
        wr_in, ce_in, ne_in, pw_in, mi_in, mo_in, fw_in, eh_in,
    )
    loads = [pltpu.make_async_copy(given[k], held[k], lsem.at[k]) for k in range(16)]
    first = (0, 2, 6)
    second = (1, 7, 3, 4, 5)
    later = (8, 9, 10, 11, 12, 13, 14, 15)
    for k in first + second + later:
        loads[k].start()

    def copy(turn, face, source, target, device):
        return pltpu.make_async_remote_copy(
            src_ref=source.at[face],
            dst_ref=target.at[face],
            send_sem=ssem.at[turn, face],
            recv_sem=rsem.at[turn, face],
            device_id=device,
            device_id_type=pl.DeviceIdType.MESH,
        )

    def send(turn, source, target, where):
        copies = [copy(turn, face, source, target, where[face]) for face in (2, 3, 0, 1)]
        for one in copies:
            one.start()
        return copies

    odd = lax.rem(my, 2)

    def send_pair(turn, pair, source, target, where):
        if pair == 2:
            ahead = 3 - odd if where is toward else 2 + odd
            copies = [
                copy(turn, ahead, source, target, (mx, lax.rem(my + 2 * odd - 1 + ny, ny))),
                copy(turn, 5 - ahead, source, target, (mx, lax.rem(my + 1 - 2 * odd + ny, ny))),
            ]
        else:
            copies = [copy(turn, face, source, target, where[face]) for face in (0, 1)]
        for one in copies:
            one.start()
        return copies

    stk[...] = jnp.zeros_like(stk)
    for k in first:
        loads[k].wait()
    for m in range(3):
        stk[m:m + 1, :] = pos_ref[0, m]
    stk[3:4, :] = spec_ref[0].astype(F32)
    own = stk[...]
    atom_id = lax.broadcasted_iota(jnp.int32, (ATOMS, GHOST), 0)
    for face in range(4):
        ghot[:, face * GHOST:(face + 1) * GHOST] = jnp.where(
            atom_id == gl_ref[0, 0, face:face + 1, :], 1.0, 0.0
        ).astype(BF16)
    lent_rows = exact_rows(own, ghot[...], mm)
    row8 = lax.broadcasted_iota(jnp.int32, (8, GHOST), 0)
    frame = (
        jnp.where(row8 == 0, -1.0, 0.0),
        jnp.where(row8 == 0, 1.0, 0.0),
        jnp.where(row8 == 1, -1.0, 0.0),
        jnp.where(row8 == 1, 1.0, 0.0),
    )
    for face in range(4):
        s1[face] = lent_rows[:, face * GHOST:(face + 1) * GHOST] + frame[face]
    pl.semaphore_wait(barrier, 4)
    sent = send(0, s1, r1, toward)

    for k in second:
        loads[k].wait()
    ghost_id = gl_ref[0, 0].astype(F32)
    mig_lane = lax.broadcasted_iota(jnp.int32, (1, GHOST), 1) // MIG
    mig_id = jnp.concatenate(
        [ml_ref[0, 0, face:face + 1, :].astype(F32) for face in range(4)]
        + [jnp.full((1, GHOST - 4 * MIG), -1.0, F32)], axis=1
    )
    atom_row = atom_id.astype(F32)
    moves = jnp.where(atom_row == mig_id, 1.0, 0.0).astype(BF16)
    mig_hot[...] = moves
    stk[...] = jnp.zeros_like(stk)
    for m in range(3):
        stk[m:m + 1, :] = vel_ref[0, m]
    speed = stk[...]
    lane8 = lax.broadcasted_iota(jnp.int32, (8, GHOST), 1) // MIG
    moved_p = exact_rows(own, moves, mm)
    moved_v = exact_rows(speed, moves, mm)
    for face in range(4):
        s5[face, 0:8, :] = jnp.where(lane8 == face, moved_p + frame[face], 0.0)
        s5[face, 8:16, :] = jnp.where(lane8 == face, moved_v, 0.0)
        s5[face, 16:17, :] = jnp.where(mig_lane == face, mig_id, -1.0)
        s5[face, 17:21, :] = ghost_id
        s5[face, 21:24, :] = jnp.zeros((3, GHOST), F32)
    sent += send(4, s5, r5, toward)

    center = cen_ref[0]
    neighbor = nei_ref[0]
    edge_id = lax.broadcasted_iota(jnp.int32, (1, EDGES), 1)
    used = edge_id < cnt_ref[0, 0]
    mask = jnp.where(used, 1.0, 0.0)
    atom_edge = lax.broadcasted_iota(jnp.int32, (ATOMS, EDGES), 0)
    chot = jnp.where(atom_edge == center, 1.0, 0.0)
    nhot = jnp.where(atom_edge == neighbor, 1.0, 0.0)
    dhot[...] = (nhot - chot).astype(BF16)
    edge_mig[...] = mm_tn(dhot[...], moves).astype(BF16)
    at_center = exact_rows(own, chot.astype(BF16), mm)
    at_neighbor = exact_rows(own, nhot.astype(BF16), mm)
    ghost_edge = lax.broadcasted_iota(jnp.int32, (4 * GHOST, EDGES), 0) + ATOMS
    nghost[...] = jnp.where(ghost_edge == neighbor, 1.0, 0.0).astype(BF16)

    row_id = jnp.where(used, center, -1).astype(F32)
    column = jnp.transpose(
        jnp.broadcast_to(jnp.where(used, center, -2).astype(F32), (128, EDGES))
    )
    neighbor_id = neighbor.astype(F32)
    for part in range(4):
        rows = slice(part * 128, part * 128 + 128)
        col = jnp.concatenate([column[rows]] * 4, axis=1)
        k0[rows, :] = jnp.where(col == row_id, ENV_SCALE, 0.0).astype(BF16)
        lmat[rows, :] = jnp.where(col == neighbor_id, ENV_SCALE, 0.0).astype(BF16)
        for face in range(4):
            mmat[rows, face * GHOST:(face + 1) * GHOST] = jnp.where(
                column[rows] == ghost_id[face:face + 1], ENV_SCALE, 0.0
            ).astype(BF16)

    for k in later:
        loads[k].wait()
    wbase[...] = jnp.zeros_like(wbase)
    wbase[0:8, :] = wr_ref[...]
    wbase[8:13, :] = ce_ref[...]
    wbase[16:21, :] = ne_ref[...]
    first_h, first_m, first_l = split3f(wbase[...])
    first_w = jnp.transpose(
        jnp.concatenate(
            [first_h, first_m, first_l, first_h[0:8], first_m[0:8], first_h[0:8], jnp.zeros((32, CH), F32)],
            axis=0,
        )
    ).astype(BF16)
    radial_w = wide4(wr_ref[...])
    product_f = [wide6_t(pw_ref[layer]) for layer in range(2)]
    product_b = [tall2(pw_ref[layer]) for layer in range(2)]
    mixin_f = [tall3(mi_ref[layer]) for layer in range(2)]
    mixin_b = [wide4_t(mi_ref[layer]) for layer in range(2)]
    mixout_f = wide6_t(mo_ref[0])
    mixout_b = wide4(mo_ref[0])
    feature_f = wide6_t(fw_ref[...])
    feature_b = wide4(fw_ref[...])
    head = eh_ref[...]
    square = lax.broadcasted_iota(jnp.int32, (CH, CH), 0) == lax.broadcasted_iota(jnp.int32, (CH, CH), 1)
    head_col = jnp.sum(jnp.where(square, head, 0.0), axis=1, keepdims=True)
    turned = jnp.sum(mo_ref[1] * head, axis=1, keepdims=True)

    for face in range(4):
        copy(0, face, s1, r1, toward[face]).wait_recv()
    ghosts = jnp.concatenate([r1[face] for face in range(4)], axis=1)
    at_neighbor = at_neighbor + exact_rows(ghosts, nghost[...], mm)
    sep = at_neighbor - at_center
    sx, sy, sz = sep[0:1], sep[1:2], sep[2:3]
    length = jnp.sqrt(sx * sx + sy * sy + sz * sz + SOFTENING)
    inv = 1.0 / length
    ux, uy, uz = sx * inv, sy * inv, sz * inv
    yrow[...] = jnp.zeros_like(yrow)
    yrow[0:1, :] = ROOT_THREE * ux
    yrow[1:2, :] = ROOT_THREE * uy
    yrow[2:3, :] = ROOT_THREE * uz
    yrow[8:9, :] = ROOT_FIFTEEN * ux * uy
    yrow[9:10, :] = ROOT_FIFTEEN * uy * uz
    yrow[10:11, :] = 0.5 * ROOT_FIVE * (3.0 * uz * uz - 1.0)
    yrow[11:12, :] = ROOT_FIFTEEN * ux * uz
    yrow[12:13, :] = 0.5 * ROOT_FIFTEEN * (ux * ux - uy * uy)
    y1h, y1m, y1l = split3f(yrow[0:8, :])
    y2h, y2m, y2l = split3f(yrow[8:16, :])
    zero8 = jnp.zeros((8, EDGES), F32)
    left = jnp.concatenate(
        [y1h, y1h, y1h, y1m, y1m, y1l, y2h, y2h, y2h, y2m, y2m, y2l] + [zero8] * 4, axis=0
    )
    left_t = jnp.transpose(left).astype(BF16)
    right1 = jnp.concatenate([y1h, y1m, y1l, y1h, y1m, y1h] + [zero8] * 10, axis=0).astype(BF16)
    right2 = jnp.concatenate(
        [zero8] * 6 + [y2h, y2m, y2l, y2h, y2m, y2h] + [zero8] * 4, axis=0
    ).astype(BF16)
    for part in range(4):
        rows = slice(part * 128, part * 128 + 128)
        same = k0[rows, :].astype(F32)
        k1h[rows, :], k1l[rows, :] = split2(same * mm(left_t[rows], right1))
        k2h[rows, :], k2l[rows, :] = split2(same * mm(left_t[rows], right2))

    basis_at = (BASIS_REACH / 7.0) * lax.broadcasted_iota(jnp.int32, (8, EDGES), 0).astype(F32)
    apart = (length - basis_at) * (1.0 / BASIS_WIDTH)
    radial = jnp.exp(-(apart * apart))
    level = lax.broadcasted_iota(jnp.int32, (8, EDGES), 0).astype(F32)
    hot_c = jnp.where(level == at_center[3:4], 1.0, 0.0)
    hot_n = jnp.where(level == at_neighbor[3:4], 1.0, 0.0)
    rad_h, rad_m, rad_l = split3f(radial)
    first_x = jnp.concatenate(
        [rad_h, hot_c, hot_n] * 3 + [rad_m, rad_m, rad_l] + [zero8] * 4, axis=0
    ).astype(BF16)
    before = mm(first_w, first_x)
    first_gate = 0.5 * (1.0 + jnp.tanh(0.5 * before))
    initial = before * first_gate

    def env(values, degree):
        three = jnp.concatenate(split3(values), axis=0)
        out = mm(three, (k0, k1h, k2h)[degree][...])
        small = out[CH:2 * CH] + out[2 * CH:]
        if degree > 0:
            low = mm(three[0:2 * CH], (None, k1l, k2l)[degree][...])
            small = small + low[0:CH] + low[CH:]
        return out[0:CH] + small

    def layer_front(hidden, layer):
        coupled = mm(product_f[layer], stack6(hidden))
        blocks = [coupled[d * CH:(d + 1) * CH] for d in range(3)]
        environ = [env(blocks[d], d) for d in range(3)]
        joined = jnp.concatenate([hidden] + [blocks[d] * environ[d] for d in range(3)], axis=0)
        inner = mm_tall3(mixin_f[layer], joined)
        gate = 0.5 * (1.0 + jnp.tanh(0.5 * inner))
        return blocks, environ, inner, gate

    def layer_back(grad_inner, grad_out, blocks, environ, layer):
        grad_joined = mm(mixin_b[layer], stack4(grad_inner))
        pulls = [grad_joined[(d + 1) * CH:(d + 2) * CH] for d in range(3)]
        scaled = [pulls[d] * blocks[d] for d in range(3)]
        grad_coupled = jnp.concatenate(
            [pulls[d] * environ[d] + env(scaled[d], d) for d in range(3)], axis=0
        )
        grad_hidden = grad_out + grad_joined[0:CH] + mm_tall2(product_b[layer], grad_coupled)
        return grad_hidden, scaled

    def pair_sums(blocks, scaled, psum):
        for d in (1, 2):
            bh, bl = split2(blocks[d])
            ah, al = split2(scaled[d])
            lhs = jnp.concatenate([bh, bl, ah, al], axis=0)
            rhs = jnp.concatenate([ah, ah, bh, bh], axis=0)
            lhs2 = jnp.concatenate([bh, ah], axis=0)
            rhs2 = jnp.concatenate([al, bl], axis=0)
            psum[d - 1] = mm_tn(lhs, rhs) + mm_tn(lhs2, rhs2)

    blocks0, environ0, inner0, gate0 = layer_front(initial, 0)
    hidden = initial + mm(mixout_f, stack6(inner0 * gate0))

    carried = mm(feature_f, stack6(hidden))
    for pair in (2, 0):
        lent = many_rows(carried, mmat[:, pair * GHOST:(pair + 2) * GHOST], mm)
        for face in (pair, pair + 1):
            s2[face] = lent[:, (face - pair) * GHOST:(face - pair + 1) * GHOST]
        sent += send_pair(1, pair, s2, r2, toward)
    combined = hidden + many_rows(carried, lmat[...], mm)
    for face in range(4):
        copy(1, face, s2, r2, toward[face]).wait_recv()
    borrowed = jnp.concatenate([r2[face] for face in range(4)], axis=1)
    combined = combined + many_rows(borrowed, nghost[...], mm)

    blocks1, environ1, inner1, gate1 = layer_front(combined, 1)
    grad_inner = turned * mask * (gate1 * (1.0 + inner1 * (1.0 - gate1)))
    grad_combined, scaled1 = layer_back(grad_inner, head_col * mask, blocks1, environ1, 1)
    for pair in (2, 0):
        back = many_rows(grad_combined, nghost[pair * GHOST:(pair + 2) * GHOST, :], mm_nt)
        for face in (pair, pair + 1):
            s3[face] = back[:, (face - pair) * GHOST:(face - pair + 1) * GHOST]
        sent += send_pair(2, pair, s3, r3, against)
    grad_carried = many_rows(grad_combined, lmat[...], mm_nt)
    pair_sums(blocks1, scaled1, psum2)
    for face in range(4):
        copy(4, face, s5, r5, toward[face]).wait_recv()
    for face in range(4):
        arrived = jnp.where(atom_row == r5[face, 16:17, :], 1.0, 0.0).astype(BF16)
        for other in range(4):
            lent_there = jnp.where(atom_row == r5[face, 17 + other:18 + other, :], 1.0, 0.0).astype(BF16)
            later_hot[face, other * GHOST:(other + 1) * GHOST, :] = mm_tn(lent_there, arrived).astype(BF16)
    landed_p = r5[0, 0:8] + r5[1, 0:8] + r5[2, 0:8] + r5[3, 0:8]
    landed_v = r5[0, 8:16] + r5[1, 8:16] + r5[2, 8:16] + r5[3, 8:16]
    landed_inverse = jnp.zeros((1, GHOST), F32)
    for kind, value in enumerate(INVERSE_MASS):
        landed_inverse = jnp.where(landed_p[3:4] == float(kind), value, landed_inverse)
    for face in range(4):
        copy(2, face, s3, r3, against[face]).wait_recv()
    returned = jnp.concatenate([r3[face] for face in range(4)], axis=1)
    grad_carried = grad_carried + many_rows(returned, mmat[...], mm_nt)
    grad_hidden = grad_combined + mm(feature_b, stack4(grad_carried))

    grad_inner = mm(mixout_b, stack4(grad_hidden)) * (gate0 * (1.0 + inner0 * (1.0 - gate0)))
    grad_initial, scaled0 = layer_back(grad_inner, grad_hidden, blocks0, environ0, 0)
    pair_sums(blocks0, scaled0, psum1)
    grad_before = grad_initial * (first_gate * (1.0 + before * (1.0 - first_gate)))
    grad_radial = mm(radial_w, stack4(grad_before))
    grad_length = jnp.sum(grad_radial * radial * apart, axis=0, keepdims=True) * (-2.0 / BASIS_WIDTH)

    grad_y = []
    for d, (yh, yl) in enumerate(((y1h, y1m), (y2h, y2m))):
        rows = jnp.concatenate([yh, yl], axis=0).astype(BF16)
        total = None
        for part in range(4):
            span = slice(part * 128, part * 128 + 128)
            pair = (psum1[d, span, :] + psum2[d, span, :]) * k0[span, :].astype(F32)
            ph, pn = split2(pair)
            one = mm(rows[:, span], ph)
            one = one[0:8] + one[8:16] + mm(rows[:, span], pn)[0:8]
            total = one if total is None else total + one
        grad_y.append(total)
    g1x, g1y, g1z = (grad_y[0][m:m + 1] for m in range(3))
    g20, g21, g22, g23, g24 = (grad_y[1][m:m + 1] for m in range(5))
    dux = ROOT_THREE * g1x + ROOT_FIFTEEN * (uy * g20 + uz * g23 + ux * g24)
    duy = ROOT_THREE * g1y + ROOT_FIFTEEN * (ux * g20 + uz * g21 - uy * g24)
    duz = ROOT_THREE * g1z + ROOT_FIFTEEN * (uy * g21 + ux * g23) + (3.0 * ROOT_FIVE) * uz * g22
    along = grad_length - inv * (dux * ux + duy * uy + duz * uz)
    grow[...] = jnp.zeros_like(grow)
    grow[0:1, :] = inv * dux + along * ux
    grow[1:2, :] = inv * duy + along * uy
    grow[2:3, :] = inv * duz + along * uz
    grad_sep = grow[...]

    back = exact_rows(grad_sep, nghost[...], mm_nt)
    leaving = exact_rows(grad_sep, edge_mig[...], mm)
    blocks = [back[:, face * GHOST:(face + 1) * GHOST] for face in range(4)]
    for face in range(4):
        s4[face, 0:8, :] = blocks[face ^ 1]
        s4[face, 8:16, :] = jnp.where(lane8 == face, leaving, 0.0)
    for k, (fx, fy) in enumerate(corners):
        s6[k, 0:8, :] = blocks[fy ^ 1]
        s6[k, 8:16, :] = blocks[fx ^ 1]

    def jump(face):
        return pltpu.make_async_remote_copy(
            src_ref=s4.at[face, pl.ds(0, 8)],
            dst_ref=r7.at[face],
            send_sem=ssem.at[6, face],
            recv_sem=rsem.at[6, face],
            device_id=straight[face],
            device_id_type=pl.DeviceIdType.MESH,
        )

    final = [jump(2), jump(3)]
    final += [copy(3, face, s4, r4, toward[face]) for face in (2, 3)]
    final += [copy(5, k, s6, r6, corner[k]) for k in range(4)]
    final += [jump(0), jump(1)]
    final += [copy(3, face, s4, r4, toward[face]) for face in (0, 1)]
    for one in final:
        one.start()
    sent += final
    grad_local = exact_rows(grad_sep, dhot[...], mm_nt)
    species = spec_ref[0]
    inverse = jnp.zeros((1, ATOMS), F32)
    for kind, value in enumerate(INVERSE_MASS):
        inverse = jnp.where(species == kind, value, inverse)
    moves = mig_hot[...]
    stays = 1.0 - mm_nt(jnp.ones((16, GHOST), BF16), moves)[0:8]
    for one in final:
        one.wait_recv()
    returned = jnp.concatenate([r4[face ^ 1, 0:8, :] for face in range(4)], axis=1)
    grad_local = grad_local + exact_rows(returned, ghot[...], mm_nt)
    grad_landed = r4[0, 8:16, :] + r4[1, 8:16, :] + r4[2, 8:16, :] + r4[3, 8:16, :]
    for face in range(4):
        parts = []
        for other in range(4):
            if other == face:
                parts.append(blocks[face])
            elif other == face ^ 1:
                parts.append(r7[face])
            elif face < 2:
                parts.append(r6[corners.index((face, other ^ 1)), 0:8, :])
            else:
                parts.append(r6[corners.index((other ^ 1, face)), 8:16, :])
        grad_landed = grad_landed + exact_rows(jnp.concatenate(parts, axis=1), later_hot[face], mm)
    velocity = speed - STEP_TIME * grad_local * inverse
    position = own + STEP_TIME * velocity
    landed_v = landed_v - STEP_TIME * grad_landed * landed_inverse
    landed_p = landed_p + STEP_TIME * landed_v
    position = position * stays + exact_rows(landed_p, moves, mm_nt)
    velocity = velocity * stays + exact_rows(landed_v, moves, mm_nt)
    for m in range(3):
        f_out[0, m] = -grad_local[m:m + 1]
        p_out[0, m] = position[m:m + 1]
        v_out[0, m] = velocity[m:m + 1]
    f_store = pltpu.make_async_copy(f_out, home.at[:, 0:3], osem.at[0])
    f_store.start()
    p_store = pltpu.make_async_copy(p_out, home.at[:, 3:6], osem.at[1])
    v_store = pltpu.make_async_copy(v_out, home.at[:, 6:9], osem.at[2])
    p_store.start()
    v_store.start()
    for one in sent:
        one.wait_send()
    for one in (f_store, p_store, v_store):
        one.wait()


def solution(mesh):
    nx, ny = mesh.shape["gx"], mesh.shape["gy"]
    placed = (
        P("gx", "gy", None, None),
        P("gx", "gy", None, None),
        P("gx", "gy", None),
        P("gx", "gy", None),
        P("gx", "gy", None),
        P("gx", "gy"),
        P("gx", "gy", None, None),
        P("gx", "gy", None, None),
        P(),
        P(),
        P(),
        P(),
        P(),
        P(),
        P(),
        P(),
    )

    def step(*operands):
        operands = list(operands)
        operands[0] = operands[0].transpose(0, 2, 1, 3)
        operands[1] = operands[1].transpose(0, 2, 1, 3)
        operands[12] = operands[12].transpose(0, 2, 1)
        operands[15] = operands[15].reshape(1, CH)
        vmem = pl.BlockSpec(memory_space=pltpu.VMEM)
        specs = [pl.BlockSpec(memory_space=pltpu.HBM)] * 16
        held = [pltpu.VMEM(one.shape, one.dtype) for one in operands]
        held[5] = pltpu.SMEM((1, 1), jnp.int32)
        big = pltpu.VMEM((EDGES, EDGES), BF16)

        def boxes(rows, width=GHOST):
            return [pltpu.VMEM((4, rows, width), F32)] * 2

        out = jax.ShapeDtypeStruct((1, 3, 1, ATOMS), F32)
        results = pl.pallas_call(
            functools.partial(kernel, nx, ny),
            out_shape=[jax.ShapeDtypeStruct((1, 9, 1, ATOMS), F32)],
            in_specs=specs,
            out_specs=[pl.BlockSpec(memory_space=pltpu.HBM)],
            scratch_shapes=[
                *[pltpu.VMEM((1, 3, 1, ATOMS), F32)] * 3,
                *held,
                pltpu.VMEM((8, ATOMS), F32),
                pltpu.VMEM((24, CH), F32),
                big, big, big, big, big, big, big, big,
                pltpu.VMEM((ATOMS, EDGES), BF16),
                pltpu.VMEM((ATOMS, EDGES), BF16),
                pltpu.VMEM((2, EDGES, EDGES), F32),
                pltpu.VMEM((2, EDGES, EDGES), F32),
                pltpu.VMEM((16, EDGES), F32),
                pltpu.VMEM((8, EDGES), F32),
                *boxes(8), *boxes(CH), *boxes(CH), *boxes(16), *boxes(24), *boxes(16),
                pltpu.VMEM((4, 8, GHOST), F32),
                pltpu.VMEM((4, EDGES, GHOST), BF16),
                pltpu.VMEM((ATOMS, GHOST), BF16),
                pltpu.VMEM((EDGES, GHOST), BF16),
                pltpu.SemaphoreType.DMA((7, 4)),
                pltpu.SemaphoreType.DMA((7, 4)),
                pltpu.SemaphoreType.DMA((16,)),
                pltpu.SemaphoreType.DMA((3,)),
            ],
            compiler_params=pltpu.CompilerParams(
                collective_id=0, has_side_effects=True, vmem_limit_bytes=60 * 1024 * 1024
            ),
        )(*operands)
        whole = results[0].transpose(0, 2, 1, 3)
        return whole[:, :, 0:3], whole[:, :, 3:6], whole[:, :, 6:9]

    face = P("gx", "gy", None, None)
    return jax.shard_map(
        step, mesh=mesh, in_specs=placed, out_specs=(face, face, face), check_vma=False
    )
```
